128 devices in a mesh: wide: 16 (over z, x_lo, core), narrow: 8 (over y, x_hi).
Axes of the slice: x: 4 (x_hi: 2, x_lo: 2; x = x_hi * 2 + x_lo), y: 4, z: 4, core: 2. Of those that a mesh axis runs over, the one named last changes fastest.
Arguments:
- tokens: bfloat16 [16384, 7168], P(('wide', 'narrow')), may hold values from -6 to 6
- grad_out: bfloat16 [16384, 7168], P(('wide', 'narrow')), may hold values from -2.5 to 2.5
- gates: bfloat16 [16384, 8], P(('wide', 'narrow')), may hold values from 0.099609375 to 1
- expert_ids: int32 [16384, 8], P(('wide', 'narrow')), may hold values from 0 to 255, as said below
- slots: int32 [16384, 8], P(('wide', 'narrow')), may hold values from 0 to 4, as said below
- w_gate: bfloat16 [16, 1792, 7168], P('wide', 'narrow'), may hold values from -0.0625 to 0.0625
- w_up: bfloat16 [16, 1792, 7168], P('wide', 'narrow'), may hold values from -0.0625 to 0.0625
- w_down: bfloat16 [16, 1792, 7168], P('wide', 'narrow'), may hold values from -0.125 to 0.125
Outputs:
- grad_tokens: bfloat16 [16384, 7168], P(('wide', 'narrow'))
- grad_gates: float32 [16384, 8], P(('wide', 'narrow'))
- grad_w_gate: bfloat16 [16, 1792, 7168], P('wide', 'narrow')
- grad_w_up: bfloat16 [16, 1792, 7168], P('wide', 'narrow')
- grad_w_down: bfloat16 [16, 1792, 7168], P('wide', 'narrow')
The draws below stay inside these ranges and needn't reach their ends.
Inputs may be any that keep to these rules, and one draw needn't show every extreme that they name: `expert_ids`: each row names 8 different experts. `slots`: for a pair whose expert is below 16, the slot is the smaller of 4 and the number of earlier pairs (row-major over token and k) of the same device's tokens with the same expert; every other pair has slot 4; slot 4 marks a pair that is not kept, so no two kept pairs of one device share an expert and a slot.
All inputs are finite; a program needn't handle non-finite values.
Results may differ from the reference program's by a relative error of at most 0.0057.
Values may be sent and summed in bfloat16 or wider, within the bound.
A program may use at most 576 MiB of HBM per device.

```python
import jax
import jax.numpy as jnp
from jax import lax

D = 7168
HID = 1792
EXPERTS = 256
TOPK = 8
TOK_DEV = 128
CAP = 4
EXPERTS_WIN = 16
TOKENS = 16384


def routing_tables(key):
    noise_key, level_key, favor_key = jax.random.split(key, 3)
    noise = jax.random.randint(noise_key, (TOKENS, EXPERTS), 0, 65536, dtype=jnp.int32)
    levels = jax.random.randint(level_key, (EXPERTS,), 0, 4, dtype=jnp.int32)
    favored = jax.random.randint(favor_key, (), 0, EXPERTS_WIN, dtype=jnp.int32)
    local_row = jnp.arange(TOKENS, dtype=jnp.int32) % TOK_DEV
    expert_row = jnp.arange(EXPERTS, dtype=jnp.int32)
    forced = ((local_row[:, None] <= CAP) & (expert_row[None, :] == favored)).astype(jnp.int32) * 1048576
    scores = (noise + levels[None, :] * 16384 + forced) * 256 + expert_row[None, :]
    chosen = lax.top_k(scores, TOPK)[1].astype(jnp.int32)
    window_hits = (chosen[:, :, None] == jnp.arange(EXPERTS_WIN, dtype=jnp.int32)[None, None, :]).astype(jnp.int32)
    blocked = window_hits.reshape(TOKENS // TOK_DEV, TOK_DEV * TOPK, EXPERTS_WIN)
    before = jnp.cumsum(blocked, axis=1) - blocked
    ranking = jnp.sum(before * blocked, axis=2).reshape(TOKENS, TOPK)
    slot_table = jnp.where(chosen < EXPERTS_WIN, jnp.minimum(ranking, CAP), CAP).astype(jnp.int32)
    return (chosen, slot_table)


def draw_expert_ids(key, part):
    chosen, slot_table = routing_tables(key)
    return chosen


def draw_slots(key, part):
    chosen, slot_table = routing_tables(key)
    return slot_table


def steps_of(rng, dims, shards, least, high):
    gain, own = 1.0, jax.random.fold_in(rng, 6)
    for axis_at, blocks in shards:
        steps = jnp.exp(jax.random.uniform(jax.random.fold_in(own, axis_at), (blocks,), jnp.float32, least / len(shards), high / len(shards)))
        gain = gain * jnp.repeat(steps, dims[axis_at] // blocks).reshape([-1 if axis == axis_at else 1 for axis in range(len(dims))])
    return gain


def scatter_about(rng, shape, spread, bound, cuts=(), kind=jnp.bfloat16):
    factor_of = steps_of(rng, shape, cuts, -0.22, 0.18) if cuts else 1.0
    drawn = jax.random.normal(rng, shape, jnp.float32) * spread * factor_of
    return jnp.minimum(jnp.maximum(drawn, -bound), bound).astype(kind)


def setup_inputs(seed: int = 0) -> dict:
    splits = jax.random.split(jax.random.key(seed), 9)
    tokens = scatter_about(splits[0], (TOKENS, D), 1.0, 6.0, ((0, 128),))
    grad_out = scatter_about(splits[1], (TOKENS, D), 0.25, 2.5, ((0, 128),))
    gates = jnp.clip(0.099609375 + 0.9003906 * jax.random.uniform(splits[2], (TOKENS, TOPK), jnp.float32) ** steps_of(splits[2], (TOKENS, TOPK), ((0, 128),), -0.2, 0.2), 0.099609375, 1.0).astype(jnp.bfloat16)
    expert_ids = draw_expert_ids(jax.random.fold_in(splits[8], 71), 0)
    slots = draw_slots(jax.random.fold_in(splits[8], 71), 0)
    w_gate = scatter_about(splits[5], (EXPERTS_WIN, HID, D), D ** -0.5, 0.0625, ((0, 16), (1, 8)))
    w_up = scatter_about(splits[6], (EXPERTS_WIN, HID, D), D ** -0.5, 0.0625, ((0, 16), (1, 8)))
    w_down = scatter_about(splits[7], (EXPERTS_WIN, HID, D), HID ** -0.5, 0.125, ((0, 16), (1, 8)))
    return {"tokens": tokens, "grad_out": grad_out, "gates": gates, "expert_ids": expert_ids, "slots": slots, "w_gate": w_gate, "w_up": w_up, "w_down": w_down}


def project(rows, weight):
    return lax.dot_general(rows, weight, (((1,), (1,)), ((), ())), preferred_element_type=jnp.float32)


def outer_sum(left, right):
    return lax.dot_general(left, right, (((0,), (0,)), ((), ())), preferred_element_type=jnp.float32)


def hidden_grads(rows_input, rows_grad, rows_weight, weight_gate, weight_up, weight_down):
    pre_gate = project(rows_input, weight_gate)
    pre_up = project(rows_input, weight_up)
    back_down = project(rows_grad, weight_down)
    sigmoid_gate = jax.nn.sigmoid(pre_gate)
    active = pre_gate * sigmoid_gate
    scaled = rows_weight[:, None] * back_down
    grad_gate = (scaled * pre_up * sigmoid_gate * (1.0 + pre_gate * (1.0 - sigmoid_gate))).astype(jnp.bfloat16)
    grad_up = (scaled * active).astype(jnp.bfloat16)
    hidden = (active * pre_up).astype(jnp.bfloat16)
    gate_part = jnp.sum(back_down * active * pre_up, axis=1)
    input_part = jnp.dot(grad_gate, weight_gate, preferred_element_type=jnp.float32) + jnp.dot(grad_up, weight_up, preferred_element_type=jnp.float32)
    scaled_grad = (rows_weight[:, None] * rows_grad.astype(jnp.float32)).astype(jnp.bfloat16)
    return grad_gate, grad_up, hidden, scaled_grad, input_part, gate_part


def reference(tokens, grad_out, gates, expert_ids, slots, w_gate, w_up, w_down):
    capacity = TOK_DEV * TOPK // EXPERTS
    blocks = TOKENS // TOK_DEV
    total_slots = blocks * capacity
    positions = jnp.arange(TOKENS, dtype=jnp.int32)
    gate_values = gates.astype(jnp.float32)

    def expert_step(carry, inputs):
        input_acc, gate_acc = carry
        expert, weight_gate, weight_up, weight_down = inputs
        matched = (expert_ids == expert) & (slots < capacity)
        target = jnp.where(matched, (positions // TOK_DEV)[:, None] * capacity + slots, total_slots).astype(jnp.int32)
        flat_target = target.reshape(-1)
        owners = jnp.broadcast_to(positions[:, None], target.shape).reshape(-1)
        owner = jnp.zeros((total_slots,), jnp.int32).at[flat_target].set(owners, mode="drop")
        filled = jnp.zeros((total_slots,), jnp.int32).at[flat_target].set(1, mode="drop")
        rows_weight = jnp.zeros((total_slots,), jnp.float32).at[flat_target].set(gate_values.reshape(-1), mode="drop")
        rows_input = jnp.where(filled[:, None] == 1, tokens[owner], jnp.zeros((), jnp.bfloat16))
        rows_grad = jnp.where(filled[:, None] == 1, grad_out[owner], jnp.zeros((), jnp.bfloat16))
        grad_gate, grad_up, hidden, scaled_grad, input_part, gate_part = hidden_grads(rows_input, rows_grad, rows_weight, weight_gate, weight_up, weight_down)
        sum_gate = outer_sum(grad_gate, rows_input).astype(jnp.bfloat16)
        sum_up = outer_sum(grad_up, rows_input).astype(jnp.bfloat16)
        sum_down = outer_sum(hidden, scaled_grad).astype(jnp.bfloat16)
        input_acc = input_acc.at[owner].add(jnp.where(filled[:, None] == 1, input_part, 0.0))
        picked = gate_part[jnp.minimum(target, total_slots - 1)]
        gate_acc = gate_acc + jnp.where(matched, picked, 0.0)
        return (input_acc, gate_acc), (sum_gate, sum_up, sum_down)

    start = (jnp.zeros((TOKENS, D), jnp.float32), jnp.zeros((TOKENS, TOPK), jnp.float32))
    inputs = (jnp.arange(EXPERTS_WIN, dtype=jnp.int32), w_gate, w_up, w_down)
    (input_acc, gate_acc), (grad_w_gate, grad_w_up, grad_w_down) = lax.scan(expert_step, start, inputs)
    return (input_acc.astype(jnp.bfloat16), gate_acc, grad_w_gate, grad_w_up, grad_w_down)
```

```python
import functools

import jax
import jax.numpy as jnp
from jax import lax
from jax.experimental import pallas as pl
from jax.experimental.pallas import tpu as pltpu
from jax.sharding import PartitionSpec as P

CAP = 4
WIDE = 16
NARROW = 8
ROWS = WIDE * CAP
CHUNKS = 8
UNITS = 2 * CHUNKS
PAD = 256
MESH = pl.DeviceIdType.MESH
F32 = jnp.float32
BF16 = jnp.bfloat16


def dot(left, right):
    return jnp.dot(left, right, preferred_element_type=F32)


def dot_nt(left, right):
    return lax.dot_general(left, right, (((1,), (1,)), ((), ())), preferred_element_type=F32)


def iota(shape, dim):
    return lax.broadcasted_iota(jnp.int32, shape, dim)


def gather_is_b(unit):
    stage, quarter = unit // 4, unit % 4
    return ((stage % 2 == 0) & (quarter % 2 == 1)) | ((stage % 2 == 1) & (quarter == 2))


def reduce_is_b(chunk):
    return (chunk % 2 == 1) & (chunk < 6)


def kernel(
    ids_ref,
    slots_ref,
    gates_ref,
    tok_hbm,
    cot_hbm,
    wg_hbm,
    wu_hbm,
    wd_hbm,
    gt_hbm,
    gg_ref,
    og_hbm,
    ou_hbm,
    od_hbm,
    place,
    place_t,
    tokbuf,
    sendbuf,
    a2abuf,
    xbuf,
    wab,
    wdn,
    acc_ab,
    acc_u,
    gsend,
    ga2a,
    gbuf,
    dd,
    dd_t,
    hq_t,
    pbuf,
    rb,
    fin,
    rbuf,
    retsend,
    retbuf,
    stage_ab,
    stage_d,
    gp,
    gpr,
    gsum,
    gret,
    tok_sem,
    w_sem,
    a2a_s,
    a2a_r,
    ga_s,
    ga_r,
    gg_s,
    gg_r,
    ag_s,
    ag_r,
    c_s,
    c_r,
    ret_s,
    ret_r,
    gp_s,
    gp_r,
    gr_s,
    gr_r,
    out_sem,
    gt_sem,
):
    w = lax.axis_index("wide")
    n = lax.axis_index("narrow")
    y, xh = n // 2, n % 2
    yp, ym, y2 = (y + 1) % 4, (y + 3) % 4, (y + 2) % 4
    ox = 1 - xh
    cw = tokbuf.shape[2]
    hid = wg_hbm.shape[1]

    def at(yy, xx):
        return yy * 2 + xx

    dev_p, dev_m, dev_x = at(yp, xh), at(ym, xh), at(y, ox)

    def cols(chunk):
        return pl.ds(pl.multiple_of(chunk * cw, 128), cw)

    def remote(src, dst, ss, rs, to_w, to_n):
        return pltpu.make_async_remote_copy(
            src_ref=src,
            dst_ref=dst,
            send_sem=ss,
            recv_sem=rs,
            device_id=(to_w, to_n),
            device_id_type=MESH,
        )

    barrier = pltpu.get_barrier_semaphore()

    @pl.loop(1, WIDE)
    def _(i):
        pl.semaphore_signal(barrier, inc=1, device_id=((w + i) % WIDE, n), device_id_type=MESH)

    @pl.loop(1, NARROW)
    def _(i):
        pl.semaphore_signal(barrier, inc=1, device_id=(w, (n + i) % NARROW), device_id_type=MESH)

    def tok_copy(half, arr, quarter):
        src = tok_hbm if arr == 0 else cot_hbm
        return pltpu.make_async_copy(
            src.at[:, cols(half * 4 + quarter)],
            tokbuf.at[half * 2 + arr, pl.ds(quarter * 128, 128)],
            tok_sem.at[half * 2 + arr, quarter],
        )

    for half in range(2):
        for arr in range(2):
            for quarter in range(4):
                tok_copy(half, arr, quarter).start()

    def w_copies(chunk):
        return (
            pltpu.make_async_copy(
                wg_hbm.at[0, :, cols(chunk)], wab.at[chunk, pl.ds(0, hid)], w_sem.at[0, chunk]
            ),
            pltpu.make_async_copy(
                wu_hbm.at[0, :, cols(chunk)], wab.at[chunk, pl.ds(PAD, hid)], w_sem.at[1, chunk]
            ),
            pltpu.make_async_copy(
                wd_hbm.at[0, :, cols(chunk)], wdn.at[chunk, pl.ds(0, hid)], w_sem.at[2, chunk]
            ),
        )

    kept = (ids_ref[...] < WIDE) & (slots_ref[...] < CAP)
    target = jnp.where(kept, ids_ref[...] * CAP + slots_ref[...], ROWS)
    row = iota((256, 128), 0)
    code = (row >> 4) * CAP + (row & 3)
    hit = jnp.zeros((256, 128), F32)
    weight = jnp.zeros((256, 128), F32)
    for k in range(8):
        match = target[k : k + 1, :] == code
        hit = hit + jnp.where(match, 1.0, 0.0)
        weight = weight + jnp.where(match, gates_ref[k : k + 1, :], 0.0)
    for q in range(4):
        part = jnp.where(((row >> 2) & 3) == q, hit, 0.0)
        place[:, q * 128 : (q + 1) * 128] = part.astype(BF16)
        place_t[q * 128 : (q + 1) * 128, :] = part.T.astype(BF16)
    gsend[...] = (
        dot(weight.astype(BF16), jnp.ones((128, 128), BF16)).astype(BF16).reshape(WIDE, 16, 128)
    )

    pl.semaphore_wait(barrier, WIDE + NARROW - 2)

    def a2a_copy(st, i):
        e = (w + i) % WIDE
        return remote(
            sendbuf.at[st, e], a2abuf.at[st, w], a2a_s.at[st, i], a2a_r.at[st, i], e, n
        )

    def ga_copy(i):
        e = (w + i) % WIDE
        return remote(gsend.at[e], ga2a.at[w], ga_s.at[i], ga_r.at[i], e, n)

    def pack(st, half, arr):
        for quarter in range(4):
            tok_copy(half, arr, quarter).wait()
        block = dot(place[...], tokbuf[st]).astype(BF16).reshape(WIDE, 16, cw)
        sendbuf[st] = block

        @pl.loop(1, WIDE)
        def _(i):
            a2a_copy(st, i).start()

        a2abuf[st, w] = sendbuf[st, w]

    for half in range(2):
        for arr in range(2):
            pack(half * 2 + arr, half, arr)
            if half == 0 and arr == 0:

                @pl.loop(1, WIDE)
                def _(i):
                    ga_copy(i).start()

                ga2a[w] = gsend[w]

                @pl.loop(0, CHUNKS)
                def _(chunk):
                    for cp in w_copies(chunk):
                        cp.start()
                    wab[chunk, hid:PAD] = jnp.zeros((PAD - hid, cw), BF16)
                    wab[chunk, PAD + hid :] = jnp.zeros((PAD - hid, cw), BF16)
                    wdn[chunk, hid:] = jnp.zeros((PAD - hid, cw), BF16)

    acc_ab[...] = jnp.zeros_like(acc_ab)
    acc_u[...] = jnp.zeros_like(acc_u)

    r2, c2 = iota((256, 256), 0), iota((256, 256), 1)
    sort_rows = (
        ((r2 >> 6) == ((c2 >> 2) & 3)) & (((r2 >> 2) & 15) == (c2 >> 4)) & ((r2 & 3) == (c2 & 3))
    )
    sort_rows = jnp.where(sort_rows, 1.0, 0.0).astype(BF16)
    unsort_rows = (
        ((c2 >> 6) == ((r2 >> 2) & 3)) & (((c2 >> 2) & 15) == (r2 >> 4)) & ((c2 & 3) == (r2 & 3))
    )
    unsort_rows = jnp.where(unsort_rows, 1.0, 0.0).astype(BF16)

    def ag_copy(u, s, piece, to_n):
        return remote(xbuf.at[u, piece], xbuf.at[u, piece], ag_s.at[u, s], ag_r.at[u, piece], w, to_n)

    def ag_half(u, s, piece, lower, sem, to_n):
        ref = xbuf.at[u, piece, pl.ds(0 if lower else 32, 32)]
        return remote(ref, ref, ag_s.at[u, s], ag_r.at[u, sem], w, to_n)

    def sends_a(u):
        return (
            (
                part(ag_copy, u, 0, n, dev_x),
                part(ag_copy, u, 1, n, dev_p),
                part(ag_copy, u, 2, n, dev_m),
            ),
            (part(ag_copy, u, 3, dev_x, dev_p), part(ag_copy, u, 4, dev_x, dev_m)),
            (part(ag_copy, u, 5, dev_m, dev_p), part(ag_copy, u, 6, at(yp, ox), dev_m)),
        )

    def sends_b(u):
        return (
            (
                part(ag_copy, u, 0, n, dev_p),
                part(ag_copy, u, 1, n, dev_m),
                part(ag_copy, u, 2, n, dev_x),
            ),
            (
                part(ag_half, u, 3, dev_m, True, dev_m, dev_p),
                part(ag_half, u, 4, dev_p, False, NARROW, dev_m),
                part(ag_copy, u, 5, dev_m, dev_x),
                part(ag_copy, u, 6, dev_p, dev_x),
            ),
            (part(ag_copy, u, 7, at(y2, xh), dev_x),),
        )

    def arrive(u, piece):
        ag_copy(u, 0, piece, dev_x).wait_recv()

    part = functools.partial

    def start_all(copies):
        for cp in copies:
            cp().start()

    def sort_stage(st):
        @pl.loop(1, WIDE)
        def _(i):
            src = (w + WIDE - i) % WIDE
            remote(
                a2abuf.at[st, src], a2abuf.at[st, src], a2a_s.at[st, i], a2a_r.at[st, i], src, n
            ).wait_recv()

        rows = dot(sort_rows, a2abuf[st].reshape(256, cw)).astype(BF16)
        for q in range(4):
            xbuf[st * 4 + q, n] = rows[q * ROWS : (q + 1) * ROWS]

    def gg_copy(i):
        return remote(gbuf.at[n], gbuf.at[n], gg_s.at[i], gg_r.at[i], w, (n + i) % NARROW)

    @pl.loop(0, UNITS + 3)
    def _(t):
        @pl.when(t < UNITS)
        def _():
            @pl.when(t % 4 == 0)
            def _():
                sort_stage(t // 4)

            @pl.when(gather_is_b(t))
            def _():
                start_all(sends_b(t)[0])

            @pl.when(jnp.logical_not(gather_is_b(t)))
            def _():
                start_all(sends_a(t)[0])

            @pl.when(t == 2)
            def _():
                @pl.loop(1, WIDE)
                def _(i):
                    src = (w + WIDE - i) % WIDE
                    remote(
                        ga2a.at[src], ga2a.at[src], ga_s.at[i], ga_r.at[i], src, n
                    ).wait_recv()

                gbuf[n] = dot(sort_rows[0:ROWS], ga2a[...].reshape(256, 128)).astype(BF16)

                @pl.loop(1, NARROW)
                def _(i):
                    gg_copy(i).start()

        u1 = t - 1

        @pl.when((u1 >= 0) & (u1 < UNITS))
        def _():
            @pl.when(gather_is_b(u1))
            def _():
                arrive(u1, dev_m)
                arrive(u1, dev_p)
                start_all(sends_b(u1)[1])

            @pl.when(jnp.logical_not(gather_is_b(u1)))
            def _():
                arrive(u1, dev_x)
                start_all(sends_a(u1)[1])

        u2 = t - 2

        @pl.when((u2 >= 0) & (u2 < UNITS))
        def _():
            @pl.when(gather_is_b(u2))
            def _():
                ag_half(u2, 0, at(y2, xh), True, at(y2, xh), dev_x).wait_recv()
                ag_half(u2, 0, at(y2, xh), False, NARROW, dev_x).wait_recv()
                start_all(sends_b(u2)[2])

            @pl.when(jnp.logical_not(gather_is_b(u2)))
            def _():
                for yy in (ym, yp):
                    arrive(u2, at(yy, xh))
                    arrive(u2, at(yy, ox))
                start_all(sends_a(u2)[2])

        u3 = t - 3

        @pl.when(u3 >= 0)
        def _():
            @pl.when(gather_is_b(u3))
            def _():
                for yy in (y, yp, ym, y2):
                    arrive(u3, at(yy, ox))

            @pl.when(jnp.logical_not(gather_is_b(u3)))
            def _():
                arrive(u3, at(y2, xh))
                arrive(u3, at(y2, ox))

            chunk = (u3 // 8) * 4 + u3 % 4
            is_cot = (u3 // 4) % 2 == 1
            rows = xbuf.at[u3]

            @pl.when(is_cot)
            def _():
                w_copies(chunk)[2].wait()
                acc_u[...] += dot_nt(rows[...].reshape(512, cw), wdn[chunk])

            @pl.when(jnp.logical_not(is_cot))
            def _():
                w_copies(chunk)[0].wait()
                w_copies(chunk)[1].wait()
                acc_ab[...] += dot_nt(rows[...].reshape(512, cw), wab[chunk])

    @pl.loop(1, NARROW)
    def _(i):
        src = (n + NARROW - i) % NARROW
        remote(gbuf.at[src], gbuf.at[src], gg_s.at[i], gg_r.at[i], w, src).wait_recv()

    gp[4:8] = jnp.zeros((4, 128), F32)
    for r in range(4):
        span = slice(r * 128, (r + 1) * 128)
        g = gbuf[2 * r : 2 * r + 2].reshape(128, 128).astype(F32)
        g = jnp.concatenate([g, g], axis=1)
        a = acc_ab[span, 0:PAD]
        b = acc_ab[span, PAD : 2 * PAD]
        u = acc_u[span, :]
        s = jax.nn.sigmoid(a)
        act = a * s
        dh = g * u
        da = dh * b * s * (1.0 + a * (1.0 - s))
        du = dh * act
        h = act * b
        dd[span, 0:PAD] = da.astype(BF16)
        dd[span, PAD : 2 * PAD] = du.astype(BF16)
        dd_t[0:PAD, span] = da.T.astype(BF16)
        dd_t[PAD : 2 * PAD, span] = du.T.astype(BF16)
        hq_t[:, span] = h.T.astype(BF16)
        gp[r : r + 1, :] = jnp.sum((u * h).T, axis=0, keepdims=True)

    def gp_copy(i):
        return remote(gp, gpr.at[n], gp_s.at[i], gp_r.at[i], w, (n + i) % NARROW)

    def gr_copy(i):
        e = (w + i) % WIDE
        return remote(gsum, gret.at[w], gr_s.at[i], gr_r.at[i], e, n)

    gpr[n] = gp[...]

    @pl.loop(1, NARROW)
    def _(i):
        gp_copy(i).start()

    lo, hi = pl.ds(0, 32), pl.ds(32, 32)

    def c_copy(k, s, piece, slot, to_n):
        return remote(pbuf.at[k, piece], rb.at[k, slot], c_s.at[k, s], c_r.at[k, s], w, to_n)

    def c_half(k, s, piece, slot, span, to_n):
        return remote(
            pbuf.at[k, piece, span], rb.at[k, slot, span], c_s.at[k, s], c_r.at[k, s], w, to_n
        )

    def add_into(k, piece, slot, span=slice(None)):
        pbuf[k, piece, span] = (
            pbuf[k, piece, span].astype(F32) + rb[k, slot, span].astype(F32)
        ).astype(BF16)

    def red_a(k):
        return (
            (
                part(c_copy, k, 0, at(y2, 0), 0, dev_p),
                part(c_copy, k, 1, at(y2, 1), 1, dev_m),
                part(c_copy, k, 3, at(yp, 1), 3, dev_p),
                part(c_copy, k, 4, at(ym, 0), 4, dev_m),
            ),
            (part(c_copy, k, 2, at(yp, 0), 2, dev_p), part(c_copy, k, 5, at(ym, 1), 5, dev_m)),
            (part(c_copy, k, 6, at(y, ox), 6, dev_x),),
        )

    def red_b(k):
        return (
            tuple(part(c_copy, k, yy, at(yy, ox), yy, dev_x) for yy in range(4)),
            (
                part(c_half, k, 4, at(y2, xh), 4, lo, dev_p),
                part(c_half, k, 5, at(y2, xh), 4, hi, dev_m),
                part(c_half, k, 7, at(yp, xh), 5, hi, dev_p),
                part(c_half, k, 8, at(ym, xh), 6, lo, dev_m),
            ),
            (
                part(c_half, k, 6, at(yp, xh), 5, lo, dev_p),
                part(c_half, k, 9, at(ym, xh), 6, hi, dev_m),
            ),
        )

    def ret_copy(h, i):
        to = (w + i) % WIDE
        return remote(
            retsend.at[h, to], retbuf.at[h, w], ret_s.at[h, i], ret_r.at[h, i], to, n
        )

    def out_copies(k, slot):
        return (
            pltpu.make_async_copy(
                stage_ab.at[slot, pl.ds(0, hid)], og_hbm.at[0, :, cols(k)], out_sem.at[slot, 0]
            ),
            pltpu.make_async_copy(
                stage_ab.at[slot, pl.ds(PAD, hid)], ou_hbm.at[0, :, cols(k)], out_sem.at[slot, 1]
            ),
            pltpu.make_async_copy(
                stage_d.at[slot, pl.ds(0, hid)], od_hbm.at[0, :, cols(k)], out_sem.at[slot, 2]
            ),
        )

    @pl.loop(0, CHUNKS + 3)
    def _(t):
        @pl.when(t < CHUNKS)
        def _():
            pbuf[t] = dot(dd[...], wab[t]).astype(BF16).reshape(NARROW, ROWS, cw)

            @pl.when(reduce_is_b(t))
            def _():
                start_all(red_b(t)[0])

            @pl.when(jnp.logical_not(reduce_is_b(t)))
            def _():
                start_all(red_a(t)[0])

        k1 = t - 1

        @pl.when((k1 >= 0) & (k1 < CHUNKS))
        def _():
            @pl.when(reduce_is_b(k1))
            def _():
                for cp in red_b(k1)[0]:
                    cp().wait_recv()
                fin[k1] = pbuf[k1, n].astype(F32) + rb[k1, y].astype(F32)
                for yy in (y2, yp, ym):
                    add_into(k1, at(yy, xh), yy)
                start_all(red_b(k1)[1])

            @pl.when(jnp.logical_not(reduce_is_b(k1)))
            def _():
                red_a(k1)[0][0]().wait_recv()
                add_into(k1, at(yp, 0), 0)
                red_a(k1)[1][0]().start()
                red_a(k1)[0][1]().wait_recv()
                add_into(k1, at(ym, 1), 1)
                red_a(k1)[1][1]().start()

        k2 = t - 2

        @pl.when((k2 >= 0) & (k2 < CHUNKS))
        def _():
            @pl.when(reduce_is_b(k2))
            def _():
                red_b(k2)[1][0]().wait_recv()
                add_into(k2, at(yp, xh), 4, lo)
                red_b(k2)[2][0]().start()
                red_b(k2)[1][1]().wait_recv()
                add_into(k2, at(ym, xh), 4, hi)
                red_b(k2)[2][1]().start()

            @pl.when(jnp.logical_not(reduce_is_b(k2)))
            def _():
                for cp in red_a(k2)[0][2:] + red_a(k2)[1]:
                    cp().wait_recv()
                fin[k2] = (
                    pbuf[k2, n].astype(F32)
                    + rb[k2, 2 + xh].astype(F32)
                    + rb[k2, 4 + xh].astype(F32)
                )
                other = at(y, ox)
                pbuf[k2, other] = (
                    pbuf[k2, other].astype(F32)
                    + rb[k2, 2 + ox].astype(F32)
                    + rb[k2, 4 + ox].astype(F32)
                ).astype(BF16)
                start_all(red_a(k2)[2])

        k3 = t - 3

        @pl.when(k3 >= 0)
        def _():
            @pl.when(reduce_is_b(k3))
            def _():
                for cp in red_b(k3)[1][2:] + red_b(k3)[2]:
                    cp().wait_recv()
                rbuf[k3] = (
                    fin[k3] + rb[k3, 5].astype(F32) + rb[k3, 6].astype(F32)
                ).astype(BF16)

            @pl.when(jnp.logical_not(reduce_is_b(k3)))
            def _():
                red_a(k3)[2][0]().wait_recv()
                rbuf[k3] = (fin[k3] + rb[k3, 6].astype(F32)).astype(BF16)

            @pl.when(k3 % 4 == 3)
            def _():
                h = k3 // 4
                rows = rbuf[pl.ds(h * 4, 4)].reshape(256, cw)
                retsend[h] = dot(unsort_rows, rows).astype(BF16).reshape(WIDE, 16, cw)

                @pl.loop(1, WIDE)
                def _(i):
                    ret_copy(h, i).start()

                retbuf[h, w] = retsend[h, w]

        @pl.when(t == 3)
        def _():
            @pl.loop(1, NARROW)
            def _(i):
                src = (n + NARROW - i) % NARROW
                remote(gpr.at[src], gpr.at[src], gp_s.at[i], gp_r.at[i], w, src).wait_recv()

            gsum[...] = jnp.sum(gpr[...], axis=0)
            gret[w] = gsum[...]

            @pl.loop(1, WIDE)
            def _(i):
                gr_copy(i).start()

        @pl.when(t < CHUNKS)
        def _():
            slot = t % 2

            @pl.when(t >= 2)
            def _():
                for cp in out_copies(t - 2, slot):
                    cp.wait()

            unit = (t // 4) * 8 + t % 4
            stage_ab[slot] = dot(dd_t[...], xbuf[unit].reshape(512, cw)).astype(BF16)

            @pl.loop(0, NARROW)
            def _(piece):
                g = gbuf[piece].astype(F32)
                g = jnp.concatenate([g] * (cw // 128), axis=1)
                tokbuf[2, pl.ds(piece * ROWS, ROWS)] = (
                    g * xbuf[unit + 4, piece].astype(F32)
                ).astype(BF16)

            stage_d[slot] = dot(hq_t[...], tokbuf[2]).astype(BF16)
            for cp in out_copies(t, slot):
                cp.start()

    @pl.loop(1, WIDE)
    def _(i):
        src = (w + WIDE - i) % WIDE
        remote(gret.at[src], gret.at[src], gr_s.at[i], gr_r.at[i], src, n).wait_recv()

    row64 = iota((ROWS, WIDE), 0)
    spread = jnp.where((row64 >> 2) == iota((ROWS, WIDE), 1), 1.0, 0.0)
    line = gret[:, n // 2, :]
    table = lax.dot_general(
        spread,
        line,
        (((1,), (0,)), ((), ())),
        precision=lax.Precision.HIGHEST,
        preferred_element_type=F32,
    )
    slot_row = iota((ROWS, 128), 0)
    lane = (n % 2) * 64 + w * CAP + (slot_row & 3)
    column = jnp.sum(
        jnp.where(iota((ROWS, 128), 1) == lane, table, 0.0), axis=1, keepdims=True
    )
    for k in range(8):
        match = target[k : k + 1, :] == slot_row
        gg_ref[k : k + 1, :] = jnp.sum(jnp.where(match, column, 0.0), axis=0, keepdims=True)

    def gt_copy(h, q):
        return pltpu.make_async_copy(
            tokbuf.at[h, pl.ds(q * 128, 128)], gt_hbm.at[:, cols(h * 4 + q)], gt_sem.at[h, q]
        )

    for h in range(2):

        @pl.loop(1, WIDE)
        def _(i):
            src = (w + WIDE - i) % WIDE
            remote(
                retbuf.at[h, src], retbuf.at[h, src], ret_s.at[h, i], ret_r.at[h, i], src, n
            ).wait_recv()

        tokbuf[h] = dot(place_t[...], retbuf[h].reshape(256, cw)).astype(BF16)
        for q in range(4):
            gt_copy(h, q).start()

    @pl.loop(1, WIDE)
    def _(i):
        for st in range(4):
            a2a_copy(st, i).wait_send()
        ga_copy(i).wait_send()
        gr_copy(i).wait_send()
        for h in range(2):
            ret_copy(h, i).wait_send()

    @pl.loop(1, NARROW)
    def _(i):
        gg_copy(i).wait_send()
        gp_copy(i).wait_send()

    @pl.loop(0, UNITS)
    def _(u):
        @pl.when(gather_is_b(u))
        def _():
            for group in sends_b(u):
                for cp in group:
                    cp().wait_send()

        @pl.when(jnp.logical_not(gather_is_b(u)))
        def _():
            for group in sends_a(u):
                for cp in group:
                    cp().wait_send()

    @pl.loop(0, CHUNKS)
    def _(k):
        @pl.when(reduce_is_b(k))
        def _():
            for group in red_b(k):
                for cp in group:
                    cp().wait_send()

        @pl.when(jnp.logical_not(reduce_is_b(k)))
        def _():
            for group in red_a(k):
                for cp in group:
                    cp().wait_send()

    for k in (CHUNKS - 2, CHUNKS - 1):
        for cp in out_copies(k, k % 2):
            cp.wait()
    for h in range(2):
        for q in range(4):
            gt_copy(h, q).wait()


def per_device(tokens, grad_out, gates, expert_ids, slots, w_gate, w_up, w_down):
    width = tokens.shape[1]
    cw = width // CHUNKS
    any_spec = pl.BlockSpec(memory_space=pl.ANY)
    vmem_spec = pl.BlockSpec(memory_space=pltpu.VMEM)
    vm = pltpu.VMEM
    dma = pltpu.SemaphoreType.DMA
    gt, gg, og, ou, od = pl.pallas_call(
        kernel,
        out_shape=(
            jax.ShapeDtypeStruct(tokens.shape, BF16),
            jax.ShapeDtypeStruct((8, 128), F32),
            jax.ShapeDtypeStruct(w_gate.shape, BF16),
            jax.ShapeDtypeStruct(w_up.shape, BF16),
            jax.ShapeDtypeStruct(w_down.shape, BF16),
        ),
        in_specs=[vmem_spec] * 3 + [any_spec] * 5,
        out_specs=(any_spec, vmem_spec, any_spec, any_spec, any_spec),
        scratch_shapes=[
            vm((256, 512), BF16),
            vm((512, 256), BF16),
            vm((4, 512, cw), BF16),
            vm((4, WIDE, 16, cw), BF16),
            vm((4, WIDE, 16, cw), BF16),
            vm((UNITS, NARROW, ROWS, cw), BF16),
            vm((CHUNKS, 2 * PAD, cw), BF16),
            vm((CHUNKS, PAD, cw), BF16),
            vm((512, 2 * PAD), F32),
            vm((512, PAD), F32),
            vm((WIDE, 16, 128), BF16),
            vm((WIDE, 16, 128), BF16),
            vm((NARROW, ROWS, 128), BF16),
            vm((512, 2 * PAD), BF16),
            vm((2 * PAD, 512), BF16),
            vm((PAD, 512), BF16),
            vm((CHUNKS, NARROW, ROWS, cw), BF16),
            vm((CHUNKS, 7, ROWS, cw), BF16),
            vm((CHUNKS, ROWS, cw), F32),
            vm((CHUNKS, ROWS, cw), BF16),
            vm((2, WIDE, 16, cw), BF16),
            vm((2, WIDE, 16, cw), BF16),
            vm((2, 2 * PAD, cw), BF16),
            vm((2, PAD, cw), BF16),
            vm((8, 128), F32),
            vm((NARROW, 8, 128), F32),
            vm((8, 128), F32),
            vm((WIDE, 8, 128), F32),
            dma((4, 4)),
            dma((3, CHUNKS)),
            dma((4, WIDE)),
            dma((4, WIDE)),
            dma((WIDE,)),
            dma((WIDE,)),
            dma((NARROW,)),
            dma((NARROW,)),
            dma((UNITS, 8)),
            dma((UNITS, NARROW + 1)),
            dma((CHUNKS, 10)),
            dma((CHUNKS, 10)),
            dma((2, WIDE)),
            dma((2, WIDE)),
            dma((NARROW,)),
            dma((NARROW,)),
            dma((WIDE,)),
            dma((WIDE,)),
            dma((2, 3)),
            dma((2, 4)),
        ],
        compiler_params=pltpu.CompilerParams(
            collective_id=0, has_side_effects=True, vmem_limit_bytes=63 * 2**20
        ),
        name="routed_backward",
    )(
        expert_ids.T,
        slots.T,
        gates.T.astype(F32),
        tokens,
        grad_out,
        w_gate,
        w_up,
        w_down,
    )
    return (gt, gg.T, og, ou, od)


def solution(mesh):
    rows = P(("wide", "narrow"), None)
    weights = P("wide", "narrow", None)
    return jax.shard_map(
        per_device,
        mesh=mesh,
        in_specs=(rows,) * 5 + (weights,) * 3,
        out_specs=(rows, rows, weights, weights, weights),
        check_vma=False,
    )
```

```python
import functools

import jax
import jax.numpy as jnp
from jax import lax
from jax.experimental import pallas as pl
from jax.experimental.pallas import tpu as pltpu
from jax.sharding import PartitionSpec as P

CAP = 4
WIDE = 16
NARROW = 8
ROWS = WIDE * CAP
STAGES = 7
CHUNKS = 2 * STAGES
UNITS = 2 * CHUNKS
GATHER_LAG = (2, 4, 6)
REDUCE_LAG = (2, 4, 6)
PAD = 256
MESH = pl.DeviceIdType.MESH
F32 = jnp.float32
BF16 = jnp.bfloat16


def dot(left, right):
    return jnp.dot(left, right, preferred_element_type=F32)


def dot_nt(left, right):
    return lax.dot_general(left, right, (((1,), (1,)), ((), ())), preferred_element_type=F32)


def iota(shape, dim):
    return lax.broadcasted_iota(jnp.int32, shape, dim)


def gather_is_b(unit):
    return (unit * 11 + 17) % 28 < 11


def reduce_is_b(chunk):
    return (chunk * 5) % 14 < 5


def kernel(
    ids_ref,
    slots_ref,
    gates_ref,
    tok_hbm,
    cot_hbm,
    wg_hbm,
    wu_hbm,
    wd_hbm,
    xq_hbm,
    ddt_hbm,
    hqt_hbm,
    placet_hbm,
    ret_hbm,
    gg_ref,
    place,
    place_t,
    tokbuf,
    sendbuf,
    a2abuf,
    xbuf,
    wab,
    wdn,
    acc_ab,
    acc_u,
    gsend,
    ga2a,
    gbuf,
    dd,
    dd_t,
    hq_t,
    pbuf,
    rb,
    fin,
    rbuf,
    retsend,
    qbuf,
    gp,
    gpr,
    gsum,
    gret,
    tok_sem,
    w_sem,
    a2a_s,
    a2a_r,
    g_s,
    g_r,
    ag_s,
    ag_r,
    c_s,
    c_r,
    ret_s,
    ret_r,
    x_sem,
    q_sem,
    out_sem,
):
    w = lax.axis_index("wide")
    n = lax.axis_index("narrow")
    y, xh = n // 2, n % 2
    yp, ym, y2 = (y + 1) % 4, (y + 3) % 4, (y + 2) % 4
    ox = 1 - xh
    cw = xbuf.shape[3]
    qw = cw // 2
    sw = 2 * cw
    hid = wg_hbm.shape[1]

    def at(yy, xx):
        return yy * 2 + xx

    xl, core = (w // 2) % 2, w % 2

    def swap(source, expert):
        return (((source // 2) % 2) ^ ((expert // 2) % 2)) & (source % 2)

    dev_p, dev_m, dev_x = at(yp, xh), at(ym, xh), at(y, ox)

    def cols(chunk):
        return pl.ds(pl.multiple_of(chunk * cw, 128), cw)

    def remote(src, dst, ss, rs, to_w, to_n):
        return pltpu.make_async_remote_copy(
            src_ref=src,
            dst_ref=dst,
            send_sem=ss,
            recv_sem=rs,
            device_id=(to_w, to_n),
            device_id_type=MESH,
        )

    barrier = pltpu.get_barrier_semaphore()

    @pl.loop(1, WIDE)
    def _(i):
        pl.semaphore_signal(barrier, inc=1, device_id=((w + i) % WIDE, n), device_id_type=MESH)

    @pl.loop(0, WIDE)
    def _(i):
        pl.semaphore_signal(barrier, inc=1, device_id=(i, at(y, ox)), device_id_type=MESH)

    @pl.loop(1, 4)
    def _(i):
        for xx in range(2):
            pl.semaphore_signal(
                barrier, inc=1, device_id=(w, at((y + i) % 4, xx)), device_id_type=MESH
            )

    def tok_copy(g, arr):
        src = tok_hbm if arr == 0 else cot_hbm
        span = pl.ds(pl.multiple_of(g * sw, 128), sw)
        return pltpu.make_async_copy(src.at[:, span], tokbuf.at[g, arr], tok_sem.at[g])

    @pl.loop(0, STAGES)
    def _(g):
        for arr in range(2):
            tok_copy(g, arr).start()

    def w_copies(chunk):
        return (
            pltpu.make_async_copy(
                wg_hbm.at[0, :, cols(chunk)], wab.at[chunk, pl.ds(0, hid)], w_sem.at[0]
            ),
            pltpu.make_async_copy(
                wu_hbm.at[0, :, cols(chunk)], wab.at[chunk, pl.ds(PAD, hid)], w_sem.at[0]
            ),
            pltpu.make_async_copy(
                wd_hbm.at[0, :, cols(chunk)], wdn.at[chunk, pl.ds(0, hid)], w_sem.at[1]
            ),
        )

    def landed(ref, sem):
        remote(ref, ref, sem, sem, w, n ^ 1).wait_recv()

    def sent(ref, sem):
        remote(ref, ref, sem, sem, w, n ^ 1).wait_send()

    def here(ref, sem):
        pltpu.make_async_copy(ref, ref, sem).wait()

    kept = (ids_ref[...] < WIDE) & (slots_ref[...] < CAP)
    target = jnp.where(kept, ids_ref[...] * CAP + slots_ref[...], ROWS)
    row = iota((256, 128), 0)
    code = (row >> 4) * CAP + (row & 3)
    gates = gates_ref[...].astype(F32)
    hit = jnp.zeros((256, 128), F32)
    weight = jnp.zeros((256, 128), F32)
    for k in range(8):
        match = target[k : k + 1, :] == code
        hit = hit + jnp.where(match, 1.0, 0.0)
        weight = weight + jnp.where(match, gates[k : k + 1, :], 0.0)
    for q in range(4):
        part = jnp.where(((row >> 2) & 3) == q, hit, 0.0)
        place[:, q * 128 : (q + 1) * 128] = part.astype(BF16)
        place_t[q * 128 : (q + 1) * 128, :] = part.T.astype(BF16)
    gsend[...] = (
        dot(weight.astype(BF16), jnp.ones((128, 128), BF16)).astype(BF16).reshape(WIDE, 16, 128)
    )

    pl.semaphore_wait(barrier, 2 * WIDE - 1 + NARROW - 2)

    def a2a_copy(g, i):
        e = (w + i) % WIDE
        return remote(
            sendbuf.at[g, e],
            a2abuf.at[g, w],
            a2a_s.at[g],
            a2a_r.at[g],
            e,
            at(y, xh ^ swap(w, e)),
        )

    def ga_copy(i):
        e = (w + i) % WIDE
        return remote(gsend.at[e], ga2a.at[w], g_s.at[0], g_r.at[0], e, at(y, xh ^ swap(w, e)))

    def pack(g):
        here(tokbuf.at[g], tok_sem.at[g])
        for arr in range(2):
            slab = jnp.concatenate(
                [tokbuf[g, arr, :, q * qw : (q + 1) * qw] for q in range(4)], axis=0
            )
            sendbuf[g, :, arr] = dot(place[...], slab).astype(BF16).reshape(WIDE, 16, qw)

        @pl.loop(1, WIDE)
        def _(i):
            a2a_copy(g, i).start()

        a2abuf[g, w] = sendbuf[g, w]

    pack(0)

    @pl.loop(1, WIDE)
    def _(i):
        ga_copy(i).start()

    ga2a[w] = gsend[w]

    @pl.loop(0, CHUNKS)
    def _(chunk):
        for cp in w_copies(chunk):
            cp.start()
        wab[chunk, hid:PAD] = jnp.zeros((PAD - hid, cw), BF16)
        wab[chunk, PAD + hid :] = jnp.zeros((PAD - hid, cw), BF16)
        wdn[chunk, hid:] = jnp.zeros((PAD - hid, cw), BF16)

    placet_copy = pltpu.make_async_copy(place_t, placet_hbm, out_sem.at[0])
    placet_copy.start()
    acc_ab[...] = jnp.zeros_like(acc_ab)
    acc_u[...] = jnp.zeros_like(acc_u)

    r2, c2 = iota((256, 256), 0), iota((256, 256), 1)
    sort_rows = (
        ((r2 >> 6) == ((c2 >> 2) & 3)) & (((r2 >> 2) & 15) == (c2 >> 4)) & ((r2 & 3) == (c2 & 3))
    )
    sort_rows = jnp.where(sort_rows, 1.0, 0.0).astype(BF16)
    unsort_rows = (
        ((c2 >> 6) == ((r2 >> 2) & 3)) & (((c2 >> 2) & 15) == (r2 >> 4)) & ((c2 & 3) == (r2 & 3))
    )
    unsort_rows = jnp.where(unsort_rows, 1.0, 0.0).astype(BF16)

    def ag_copy(u, s, piece, to_n):
        ref = xbuf.at[u, piece]
        return remote(ref, ref, ag_s.at[u // 7], ag_r.at[u, s], w, to_n)

    def ag_half(u, s, piece, lower, to_n):
        ref = xbuf.at[u, piece, pl.ds(0 if lower else 32, 32)]
        return remote(ref, ref, ag_s.at[u // 7], ag_r.at[u, s], w, to_n)

    part = functools.partial

    def sends_a(u):
        return (
            (
                part(ag_copy, u, 0, n, dev_x),
                part(ag_copy, u, 1, n, dev_p),
                part(ag_copy, u, 1, n, dev_m),
            ),
            (part(ag_copy, u, 1, dev_x, dev_p), part(ag_copy, u, 1, dev_x, dev_m)),
            (part(ag_copy, u, 2, dev_m, dev_p), part(ag_copy, u, 2, at(yp, ox), dev_m)),
        )

    def sends_b(u):
        return (
            (
                part(ag_copy, u, 0, n, dev_p),
                part(ag_copy, u, 0, n, dev_m),
                part(ag_copy, u, 2, n, dev_x),
            ),
            (
                part(ag_half, u, 1, dev_m, True, dev_p),
                part(ag_half, u, 1, dev_p, False, dev_m),
                part(ag_copy, u, 2, dev_m, dev_x),
                part(ag_copy, u, 2, dev_p, dev_x),
            ),
            (part(ag_copy, u, 2, at(y2, xh), dev_x),),
        )

    def start_all(copies):
        for cp in copies:
            cp().start()

    def sort_stage(g):
        landed(a2abuf.at[g, pl.ds(0, WIDE - 1)], a2a_r.at[g])
        for arr in range(2):
            rows = dot(sort_rows, a2abuf[g, :, arr].reshape(256, qw)).astype(BF16)
            for q in range(4):
                xbuf[g * 4 + arr * 2 + q // 2, n, :, (q % 2) * qw : (q % 2 + 1) * qw] = rows[
                    q * ROWS : (q + 1) * ROWS
                ]

    def gg_copy(i):
        return remote(gbuf.at[n], gbuf.at[n], g_s.at[1], g_r.at[1], w, (n + i) % NARROW)

    def x_copy(u):
        return pltpu.make_async_copy(xbuf.at[u], xq_hbm.at[u], x_sem.at[0])

    def q_copy(u):
        return pltpu.make_async_copy(qbuf.at[u % 2], xq_hbm.at[u], q_sem.at[u % 2])

    lag1, lag2, lag3 = GATHER_LAG

    @pl.loop(0, UNITS + lag3)
    def _(t):
        @pl.when(t < UNITS)
        def _():
            @pl.when(t % 4 == 0)
            def _():
                sort_stage(t // 4)

            @pl.when(gather_is_b(t))
            def _():
                start_all(sends_b(t)[0])

            @pl.when(jnp.logical_not(gather_is_b(t)))
            def _():
                start_all(sends_a(t)[0])

        @pl.when(t == 0)
        def _():
            pack(1)

        @pl.when((t % 4 == 1) & (t // 4 + 2 < STAGES))
        def _():
            pack(t // 4 + 2)

        @pl.when(t == 3)
        def _():
            landed(ga2a.at[pl.ds(0, WIDE - 1)], g_r.at[0])
            gbuf[n] = dot(sort_rows[0:ROWS], ga2a[...].reshape(256, 128)).astype(BF16)

            @pl.loop(1, NARROW)
            def _(i):
                gg_copy(i).start()

        @pl.when(t == lag3)
        def _():
            landed(gbuf.at[pl.ds(0, NARROW - 1)], g_r.at[1])
            here(wab.at[:, pl.ds(0, 2 * hid)], w_sem.at[0])
            here(wdn.at[:, pl.ds(0, hid)], w_sem.at[1])

        u1 = t - lag1

        @pl.when((u1 >= 0) & (u1 < UNITS))
        def _():
            @pl.when(gather_is_b(u1))
            def _():
                landed(xbuf.at[u1, pl.ds(0, 2)], ag_r.at[u1, 0])
                start_all(sends_b(u1)[1])

            @pl.when(jnp.logical_not(gather_is_b(u1)))
            def _():
                landed(xbuf.at[u1, 0], ag_r.at[u1, 0])
                start_all(sends_a(u1)[1])

        u2 = t - lag2

        @pl.when((u2 >= 0) & (u2 < UNITS))
        def _():
            @pl.when(gather_is_b(u2))
            def _():
                landed(xbuf.at[u2, 0], ag_r.at[u2, 1])
                start_all(sends_b(u2)[2])

            @pl.when(jnp.logical_not(gather_is_b(u2)))
            def _():
                landed(xbuf.at[u2, pl.ds(0, 4)], ag_r.at[u2, 1])
                start_all(sends_a(u2)[2])

        u3 = t - lag3

        @pl.when(u3 >= 0)
        def _():
            @pl.when(gather_is_b(u3))
            def _():
                landed(xbuf.at[u3, pl.ds(0, 4)], ag_r.at[u3, 2])

            @pl.when(jnp.logical_not(gather_is_b(u3)))
            def _():
                landed(xbuf.at[u3, pl.ds(0, 2)], ag_r.at[u3, 2])

            chunk = (u3 // 4) * 2 + u3 % 2
            is_cot = (u3 // 2) % 2 == 1

            @pl.when(is_cot)
            def _():
                acc_u[...] += dot_nt(xbuf[u3].reshape(512, cw), wdn[chunk])

                @pl.when(chunk >= 2)
                def _():
                    q_copy(u3).wait()

                @pl.loop(0, NARROW)
                def _(piece):
                    g = gbuf[piece].astype(F32)
                    g = jnp.concatenate([g] * (cw // 128), axis=1)
                    qbuf[u3 % 2, piece] = (g * xbuf[u3, piece].astype(F32)).astype(BF16)

                q_copy(u3).start()

            @pl.when(jnp.logical_not(is_cot))
            def _():
                x_copy(u3).start()
                acc_ab[...] += dot_nt(xbuf[u3].reshape(512, cw), wab[chunk])

    def hidden(r):
        span = slice(r * 128, (r + 1) * 128)
        g = gbuf[2 * r : 2 * r + 2].reshape(128, 128).astype(F32)
        g = jnp.concatenate([g, g], axis=1)
        a = acc_ab[span, 0:PAD]
        b = acc_ab[span, PAD : 2 * PAD]
        u = acc_u[span, :]
        s = jax.nn.sigmoid(a)
        act = a * s
        dh = g * u
        da = dh * b * s * (1.0 + a * (1.0 - s))
        du = dh * act
        h = act * b
        dd[span, 0:PAD] = da.astype(BF16)
        dd[span, PAD : 2 * PAD] = du.astype(BF16)
        acc_ab[span, 0:PAD] = h
        acc_u[span, :] = u * h

    for r in range(4):
        hidden(r)

    ddt_copy = pltpu.make_async_copy(dd_t, ddt_hbm, out_sem.at[1])
    hqt_copy = pltpu.make_async_copy(hq_t, hqt_hbm, out_sem.at[2])

    def turn():
        gp[4:8] = jnp.zeros((4, 128), F32)
        for r in range(4):
            span = slice(r * 128, (r + 1) * 128)
            dd_t[:, span] = dd[span, :].astype(F32).T.astype(BF16)
            hq_t[:, span] = acc_ab[span, 0:PAD].T.astype(BF16)
            gp[r : r + 1, :] = jnp.sum(acc_u[span, :].T, axis=0, keepdims=True)
        ddt_copy.start()
        hqt_copy.start()
        gpr[n] = gp[...]

        @pl.loop(1, NARROW)
        def _(i):
            gp_copy(i).start()

    def gp_copy(i):
        return remote(gp, gpr.at[n], g_s.at[2], g_r.at[2], w, (n + i) % NARROW)

    def gr_copy(i):
        e = (w + i) % WIDE
        return remote(gsum, gret.at[w], g_s.at[3], g_r.at[3], e, n)

    lo, hi = pl.ds(0, 32), pl.ds(32, 32)

    def c_copy(k, s, piece, slot, to_n):
        return remote(
            pbuf.at[k, piece], rb.at[k, slot], c_s.at[k // 7], c_r.at[k, s], w, to_n
        )

    def c_half(k, s, piece, slot, span, to_n):
        return remote(
            pbuf.at[k, piece, span], rb.at[k, slot, span], c_s.at[k // 7], c_r.at[k, s], w, to_n
        )

    def add_into(k, piece, slot, span=slice(None)):
        pbuf[k, piece, span] = (
            pbuf[k, piece, span].astype(F32) + rb[k, slot, span].astype(F32)
        ).astype(BF16)

    def red_a(k):
        return (
            (
                part(c_copy, k, 0, at(y2, 0), 0, dev_p),
                part(c_copy, k, 0, at(y2, 1), 1, dev_m),
                part(c_copy, k, 1, at(yp, 1), 3, dev_p),
                part(c_copy, k, 1, at(ym, 0), 4, dev_m),
            ),
            (
                part(c_copy, k, 1, at(yp, 0), 2, dev_p),
                part(c_copy, k, 1, at(ym, 1), 5, dev_m),
            ),
            (part(c_copy, k, 2, at(y, ox), 6, dev_x),),
        )

    def red_b(k):
        return (
            tuple(part(c_copy, k, 0, at(yy, ox), yy, dev_x) for yy in range(4)),
            (
                part(c_half, k, 1, at(y2, xh), 4, lo, dev_p),
                part(c_half, k, 1, at(y2, xh), 4, hi, dev_m),
                part(c_half, k, 2, at(yp, xh), 5, hi, dev_p),
                part(c_half, k, 2, at(ym, xh), 6, lo, dev_m),
            ),
            (
                part(c_half, k, 2, at(yp, xh), 5, lo, dev_p),
                part(c_half, k, 2, at(ym, xh), 6, hi, dev_m),
            ),
        )

    def ret_copy(g, i):
        to = (w + i) % WIDE
        return remote(
            retsend.at[g, to],
            ret_hbm.at[g, w],
            ret_s.at[g],
            ret_r.at[g],
            to,
            at(y, xh ^ swap(to, w)),
        )

    def own_copy(g):
        return pltpu.make_async_copy(retsend.at[g, w], ret_hbm.at[g, w], out_sem.at[3])

    clag1, clag2, clag3 = REDUCE_LAG

    @pl.loop(0, CHUNKS + clag3)
    def _(t):
        @pl.when(t < CHUNKS)
        def _():
            pbuf[t] = dot(dd[...], wab[t]).astype(BF16).reshape(NARROW, ROWS, cw)

            @pl.when(reduce_is_b(t))
            def _():
                start_all(red_b(t)[0])

            @pl.when(jnp.logical_not(reduce_is_b(t)))
            def _():
                start_all(red_a(t)[0])

        k1 = t - clag1

        @pl.when((k1 >= 0) & (k1 < CHUNKS))
        def _():
            @pl.when(reduce_is_b(k1))
            def _():
                landed(rb.at[k1, pl.ds(0, 4)], c_r.at[k1, 0])
                for yy in (y2, yp, ym):
                    add_into(k1, at(yy, xh), yy)
                start_all(red_b(k1)[1])
                fin[k1] = pbuf[k1, n].astype(F32) + rb[k1, y].astype(F32)

            @pl.when(jnp.logical_not(reduce_is_b(k1)))
            def _():
                landed(rb.at[k1, pl.ds(0, 2)], c_r.at[k1, 0])
                add_into(k1, at(yp, 0), 0)
                add_into(k1, at(ym, 1), 1)
                start_all(red_a(k1)[1])

        k2 = t - clag2

        @pl.when((k2 >= 0) & (k2 < CHUNKS))
        def _():
            @pl.when(reduce_is_b(k2))
            def _():
                landed(rb.at[k2, 4], c_r.at[k2, 1])
                add_into(k2, at(yp, xh), 4, lo)
                add_into(k2, at(ym, xh), 4, hi)
                start_all(red_b(k2)[2])

            @pl.when(jnp.logical_not(reduce_is_b(k2)))
            def _():
                landed(rb.at[k2, pl.ds(2, 4)], c_r.at[k2, 1])
                other = at(y, ox)
                pbuf[k2, other] = (
                    pbuf[k2, other].astype(F32)
                    + rb[k2, 2 + ox].astype(F32)
                    + rb[k2, 4 + ox].astype(F32)
                ).astype(BF16)
                start_all(red_a(k2)[2])
                fin[k2] = (
                    pbuf[k2, n].astype(F32)
                    + rb[k2, 2 + xh].astype(F32)
                    + rb[k2, 4 + xh].astype(F32)
                )

        k3 = t - clag3

        @pl.when(k3 >= 0)
        def _():
            @pl.when(reduce_is_b(k3))
            def _():
                landed(rb.at[k3, pl.ds(5, 2)], c_r.at[k3, 2])
                rbuf[k3] = (
                    fin[k3] + rb[k3, 5].astype(F32) + rb[k3, 6].astype(F32)
                ).astype(BF16)

            @pl.when(jnp.logical_not(reduce_is_b(k3)))
            def _():
                landed(rb.at[k3, 6], c_r.at[k3, 2])
                rbuf[k3] = (fin[k3] + rb[k3, 6].astype(F32)).astype(BF16)

            @pl.when(k3 % 2 == 1)
            def _():
                g = k3 // 2
                rows = jnp.concatenate(
                    [
                        rbuf[2 * g + q // 2, :, (q % 2) * qw : (q % 2 + 1) * qw]
                        for q in range(4)
                    ],
                    axis=0,
                )
                retsend[g] = dot(unsort_rows, rows).astype(BF16).reshape(WIDE, 16, qw)

                @pl.loop(1, WIDE)
                def _(i):
                    ret_copy(g, i).start()

                own_copy(g).start()

        @pl.when(t == 1)
        def _():
            turn()

        @pl.when(t == 6)
        def _():
            landed(gpr.at[pl.ds(0, NARROW - 1)], g_r.at[2])
            gsum[...] = jnp.sum(gpr[...], axis=0)
            gret[w] = gsum[...]

            @pl.loop(1, WIDE)
            def _(i):
                gr_copy(i).start()

    landed(gret.at[pl.ds(0, WIDE - 1)], g_r.at[3])

    row64 = iota((ROWS, WIDE), 0)
    spread = jnp.where((row64 >> 2) == iota((ROWS, WIDE), 1), 1.0, 0.0)
    line = gret[:, y, :]
    table = lax.dot_general(
        spread,
        line,
        (((1,), (0,)), ((), ())),
        precision=lax.Precision.HIGHEST,
        preferred_element_type=F32,
    )
    slot_row = iota((ROWS, 128), 0)
    turned = (((slot_row >> 3) & 1) ^ xl) & core
    lane = (xh ^ turned) * ROWS + w * CAP + (slot_row & 3)
    column = jnp.sum(
        jnp.where(iota((ROWS, 128), 1) == lane, table, 0.0), axis=1, keepdims=True
    )
    for k in range(8):
        match = target[k : k + 1, :] == slot_row
        gg_ref[k : k + 1, :] = jnp.sum(jnp.where(match, column, 0.0), axis=0, keepdims=True)

    sent(gsend.at[pl.ds(0, WIDE - 1)], g_s.at[0])
    sent(gbuf.at[pl.ds(0, NARROW - 1)], g_s.at[1])
    sent(gpr.at[pl.ds(0, NARROW - 1)], g_s.at[2])
    sent(gret.at[pl.ds(0, WIDE - 1)], g_s.at[3])
    for i in range(4):
        sent(xbuf.at[pl.ds(i * 7, 7), pl.ds(0, 7)], ag_s.at[i])
    for i in range(2):
        sent(pbuf.at[pl.ds(i * 7, 7), pl.ds(0, 7)], c_s.at[i])
    here(xbuf.at[pl.ds(0, CHUNKS)], x_sem.at[0])
    for k in range(2):
        q_copy(UNITS - 2 + k).wait()
    placet_copy.wait()
    ddt_copy.wait()
    hqt_copy.wait()

    @pl.loop(0, STAGES)
    def _(g):
        sent(sendbuf.at[g, pl.ds(0, WIDE - 1)], a2a_s.at[g])
        sent(retsend.at[g, pl.ds(0, WIDE - 1)], ret_s.at[g])
        landed(retsend.at[g, pl.ds(0, WIDE - 1)], ret_r.at[g])

    here(retsend.at[:, 0], out_sem.at[3])


def finish(
    ddt_ref, hqt_ref, placet_ref, gg_ref, ret_ref, x_ref, q_ref, gt_ref, gg_out, og_ref, ou_ref, od_ref
):
    hid = og_ref.shape[1]
    cw = x_ref.shape[2]
    qw = cw // 2
    for half in range(2):
        span = slice(half * cw, (half + 1) * cw)
        both = dot(ddt_ref[...], x_ref[half]).astype(BF16)
        og_ref[0, :, span] = both[0:hid]
        ou_ref[0, :, span] = both[PAD : PAD + hid]
        od_ref[0, :, span] = dot(hqt_ref[...], q_ref[half]).astype(BF16)[0:hid]
    home = dot(placet_ref[...], ret_ref[0]).astype(BF16)
    for q in range(4):
        gt_ref[:, q * qw : (q + 1) * qw] = home[q * 128 : (q + 1) * 128]
    gg_out[...] = gg_ref[...]


def per_device(tokens, grad_out, gates, expert_ids, slots, w_gate, w_up, w_down):
    width = tokens.shape[1]
    cw = width // CHUNKS
    any_spec = pl.BlockSpec(memory_space=pl.ANY)
    vmem_spec = pl.BlockSpec(memory_space=pltpu.VMEM)
    vm = pltpu.VMEM
    dma = pltpu.SemaphoreType.DMA
    sds = jax.ShapeDtypeStruct
    xq, ddt, hqt, placet, ret, gg = pl.pallas_call(
        kernel,
        out_shape=(
            sds((UNITS, NARROW, ROWS, cw), BF16),
            sds((2 * PAD, 512), BF16),
            sds((PAD, 512), BF16),
            sds((512, 256), BF16),
            sds((STAGES, WIDE, 16, cw // 2), BF16),
            sds((8, 128), F32),
        ),
        in_specs=[vmem_spec] * 3 + [any_spec] * 5,
        out_specs=(any_spec,) * 5 + (vmem_spec,),
        scratch_shapes=[
            vm((256, 512), BF16),
            vm((512, 256), BF16),
            vm((STAGES, 2, 128, 2 * cw), BF16),
            vm((STAGES, WIDE, 2, 16, cw // 2), BF16),
            vm((STAGES, WIDE, 2, 16, cw // 2), BF16),
            vm((UNITS, NARROW, ROWS, cw), BF16),
            vm((CHUNKS, 2 * PAD, cw), BF16),
            vm((CHUNKS, PAD, cw), BF16),
            vm((512, 2 * PAD), F32),
            vm((512, PAD), F32),
            vm((WIDE, 16, 128), BF16),
            vm((WIDE, 16, 128), BF16),
            vm((NARROW, ROWS, 128), BF16),
            vm((512, 2 * PAD), BF16),
            vm((2 * PAD, 512), BF16),
            vm((PAD, 512), BF16),
            vm((CHUNKS, NARROW, ROWS, cw), BF16),
            vm((CHUNKS, 7, ROWS, cw), BF16),
            vm((CHUNKS, ROWS, cw), F32),
            vm((CHUNKS, ROWS, cw), BF16),
            vm((STAGES, WIDE, 16, cw // 2), BF16),
            vm((2, NARROW, ROWS, cw), BF16),
            vm((8, 128), F32),
            vm((NARROW, 8, 128), F32),
            vm((8, 128), F32),
            vm((WIDE, 8, 128), F32),
            dma((STAGES,)),
            dma((2,)),
            dma((STAGES,)),
            dma((STAGES,)),
            dma((4,)),
            dma((4,)),
            dma((4,)),
            dma((UNITS, 3)),
            dma((2,)),
            dma((CHUNKS, 3)),
            dma((STAGES,)),
            dma((STAGES,)),
            dma((1,)),
            dma((2,)),
            dma((4,)),
        ],
        compiler_params=pltpu.CompilerParams(
            collective_id=0, has_side_effects=True, vmem_limit_bytes=63 * 2**20
        ),
        name="routed_backward",
    )(
        expert_ids.T,
        slots.T,
        gates.T,
        tokens,
        grad_out,
        w_gate,
        w_up,
        w_down,
    )
    xq = xq.reshape(UNITS, 512, cw)
    ret = ret.reshape(STAGES, 256, cw // 2)
    hid = w_gate.shape[1]

    def whole(shape):
        return pl.BlockSpec(shape, lambda g: (0,) * len(shape))

    weight_block = pl.BlockSpec((1, hid, 2 * cw), lambda g: (0, 0, g))
    gt, gg, og, ou, od = pl.pallas_call(
        finish,
        grid=(STAGES,),
        in_specs=[
            whole((2 * PAD, 512)),
            whole((PAD, 512)),
            whole((512, 256)),
            whole((8, 128)),
            pl.BlockSpec((1, 256, cw // 2), lambda g: (g, 0, 0)),
            pl.BlockSpec((2, 512, cw), lambda g: (2 * g, 0, 0)),
            pl.BlockSpec((2, 512, cw), lambda g: (2 * g + 1, 0, 0)),
        ],
        out_specs=[
            pl.BlockSpec((128, 2 * cw), lambda g: (0, g)),
            whole((8, 128)),
            weight_block,
            weight_block,
            weight_block,
        ],
        out_shape=[
            sds(tokens.shape, BF16),
            sds((8, 128), F32),
            sds(w_gate.shape, BF16),
            sds(w_up.shape, BF16),
            sds(w_down.shape, BF16),
        ],
        compiler_params=pltpu.CompilerParams(vmem_limit_bytes=62 * 2**20),
        name="weight_grads",
    )(ddt, hqt, placet, gg, ret, xq, xq)
    return (gt, gg.T, og, ou, od)


def solution(mesh):
    rows = P(("wide", "narrow"), None)
    weights = P("wide", "narrow", None)
    return jax.shard_map(
        per_device,
        mesh=mesh,
        in_specs=(rows,) * 5 + (weights,) * 3,
        out_specs=(rows, rows, weights, weights, weights),
        check_vma=False,
    )
```

```python
import functools

import jax
import jax.numpy as jnp
from jax import lax
from jax.experimental import pallas as pl
from jax.experimental.pallas import tpu as pltpu
from jax.sharding import PartitionSpec as P

CAP = 4
WIDE = 16
NARROW = 8
ROWS = WIDE * CAP
STAGES = 7
CHUNKS = 2 * STAGES
UNITS = 2 * CHUNKS
GATHER_LAG = (2, 4, 6)
REDUCE_LAG = (4, 8, 12)
GRADS_LAG = 3
PAD = 256
MESH = pl.DeviceIdType.MESH
F32 = jnp.float32
BF16 = jnp.bfloat16


def dot(left, right):
    return jnp.dot(left, right, preferred_element_type=F32)


def dot_nt(left, right):
    return lax.dot_general(left, right, (((1,), (1,)), ((), ())), preferred_element_type=F32)


def iota(shape, dim):
    return lax.broadcasted_iota(jnp.int32, shape, dim)


def gather_is_b(unit):
    return (unit * 11) % 28 < 11


def reduce_is_b(chunk):
    return (chunk * 5 + 9) % 14 < 5


def kernel(
    ids_ref,
    slots_ref,
    gates_ref,
    tok_hbm,
    cot_hbm,
    wg_hbm,
    wu_hbm,
    wd_hbm,
    og_hbm,
    ou_hbm,
    od_hbm,
    placet_hbm,
    ret_hbm,
    gg_ref,
    place,
    place_t,
    tokbuf,
    sendbuf,
    a2abuf,
    xbuf,
    wab,
    wdn,
    acc_ab,
    acc_u,
    gsend,
    ga2a,
    gbuf,
    dd,
    dd_t,
    hq_t,
    pbuf,
    rb,
    fin,
    rbuf,
    retsend,
    qbuf,
    stage_ab,
    stage_d,
    gp,
    gpr,
    gsum,
    gret,
    tok_sem,
    w_sem,
    a2a_s,
    a2a_r,
    g_s,
    g_r,
    ag_s,
    ag_r,
    c_s,
    c_r,
    ret_s,
    ret_r,
    grad_sem,
    out_sem,
):
    w = lax.axis_index("wide")
    n = lax.axis_index("narrow")
    y, xh = n // 2, n % 2
    yp, ym, y2 = (y + 1) % 4, (y + 3) % 4, (y + 2) % 4
    ox = 1 - xh
    cw = xbuf.shape[3]
    qw = cw // 2
    sw = 2 * cw
    hid = wg_hbm.shape[1]

    def at(yy, xx):
        return yy * 2 + xx

    xl, core = (w // 2) % 2, w % 2

    def swap(source, expert):
        return (((source // 2) % 2) ^ ((expert // 2) % 2)) & (source % 2)

    dev_p, dev_m, dev_x = at(yp, xh), at(ym, xh), at(y, ox)

    def cols(chunk):
        return pl.ds(pl.multiple_of(chunk * cw, 128), cw)

    def remote(src, dst, ss, rs, to_w, to_n):
        return pltpu.make_async_remote_copy(
            src_ref=src,
            dst_ref=dst,
            send_sem=ss,
            recv_sem=rs,
            device_id=(to_w, to_n),
            device_id_type=MESH,
        )

    barrier = pltpu.get_barrier_semaphore()

    @pl.loop(1, WIDE)
    def _(i):
        pl.semaphore_signal(barrier, inc=1, device_id=((w + i) % WIDE, n), device_id_type=MESH)

    @pl.loop(0, WIDE)
    def _(i):
        pl.semaphore_signal(barrier, inc=1, device_id=(i, at(y, ox)), device_id_type=MESH)

    @pl.loop(1, 4)
    def _(i):
        for xx in range(2):
            pl.semaphore_signal(
                barrier, inc=1, device_id=(w, at((y + i) % 4, xx)), device_id_type=MESH
            )

    def tok_copy(g, arr):
        src = tok_hbm if arr == 0 else cot_hbm
        span = pl.ds(pl.multiple_of(g * sw, 128), sw)
        return pltpu.make_async_copy(src.at[:, span], tokbuf.at[g, arr], tok_sem.at[g])

    @pl.loop(0, STAGES)
    def _(g):
        for arr in range(2):
            tok_copy(g, arr).start()

    def w_copies(chunk):
        return (
            pltpu.make_async_copy(
                wg_hbm.at[0, :, cols(chunk)], wab.at[chunk, pl.ds(0, hid)], w_sem.at[0]
            ),
            pltpu.make_async_copy(
                wu_hbm.at[0, :, cols(chunk)], wab.at[chunk, pl.ds(PAD, hid)], w_sem.at[0]
            ),
            pltpu.make_async_copy(
                wd_hbm.at[0, :, cols(chunk)], wdn.at[chunk, pl.ds(0, hid)], w_sem.at[1]
            ),
        )

    def landed(ref, sem):
        remote(ref, ref, sem, sem, w, n ^ 1).wait_recv()

    def sent(ref, sem):
        remote(ref, ref, sem, sem, w, n ^ 1).wait_send()

    def here(ref, sem):
        pltpu.make_async_copy(ref, ref, sem).wait()

    kept = (ids_ref[...] < WIDE) & (slots_ref[...] < CAP)
    target = jnp.where(kept, ids_ref[...] * CAP + slots_ref[...], ROWS)
    row = iota((256, 128), 0)
    code = (row >> 4) * CAP + (row & 3)
    gates = gates_ref[...].astype(F32)
    hit = jnp.zeros((256, 128), F32)
    weight = jnp.zeros((256, 128), F32)
    for k in range(8):
        match = target[k : k + 1, :] == code
        hit = hit + jnp.where(match, 1.0, 0.0)
        weight = weight + jnp.where(match, gates[k : k + 1, :], 0.0)
    for q in range(4):
        part = jnp.where(((row >> 2) & 3) == q, hit, 0.0)
        place[:, q * 128 : (q + 1) * 128] = part.astype(BF16)
        place_t[q * 128 : (q + 1) * 128, :] = part.T.astype(BF16)
    gsend[...] = (
        dot(weight.astype(BF16), jnp.ones((128, 128), BF16)).astype(BF16).reshape(WIDE, 16, 128)
    )

    def a2a_copy(g, i):
        e = (w + i) % WIDE
        return remote(
            sendbuf.at[g, e],
            a2abuf.at[g, w],
            a2a_s.at[g],
            a2a_r.at[g],
            e,
            at(y, xh ^ swap(w, e)),
        )

    def ga_copy(i):
        e = (w + i) % WIDE
        return remote(gsend.at[e], ga2a.at[w], g_s.at[0], g_r.at[0], e, at(y, xh ^ swap(w, e)))

    def pack(g):
        here(tokbuf.at[g], tok_sem.at[g])
        for arr in range(2):
            slab = jnp.concatenate(
                [tokbuf[g, arr, :, q * qw : (q + 1) * qw] for q in range(4)], axis=0
            )
            sendbuf[g, :, arr] = dot(place[...], slab).astype(BF16).reshape(WIDE, 16, qw)

    def post(g):
        @pl.loop(1, WIDE)
        def _(i):
            a2a_copy(g, i).start()

        a2abuf[g, w] = sendbuf[g, w]

    pack(0)
    pl.semaphore_wait(barrier, 2 * WIDE - 1 + NARROW - 2)
    post(0)

    @pl.loop(1, WIDE)
    def _(i):
        ga_copy(i).start()

    ga2a[w] = gsend[w]

    @pl.loop(0, CHUNKS)
    def _(chunk):
        for cp in w_copies(chunk):
            cp.start()
        wab[chunk, hid:PAD] = jnp.zeros((PAD - hid, cw), BF16)
        wab[chunk, PAD + hid :] = jnp.zeros((PAD - hid, cw), BF16)
        wdn[chunk, hid:] = jnp.zeros((PAD - hid, cw), BF16)

    placet_copy = pltpu.make_async_copy(place_t, placet_hbm, out_sem.at[0])
    placet_copy.start()
    acc_ab[...] = jnp.zeros_like(acc_ab)
    acc_u[...] = jnp.zeros_like(acc_u)

    r2, c2 = iota((256, 256), 0), iota((256, 256), 1)
    sort_rows = (
        ((r2 >> 6) == ((c2 >> 2) & 3)) & (((r2 >> 2) & 15) == (c2 >> 4)) & ((r2 & 3) == (c2 & 3))
    )
    sort_rows = jnp.where(sort_rows, 1.0, 0.0).astype(BF16)
    unsort_rows = (
        ((c2 >> 6) == ((r2 >> 2) & 3)) & (((c2 >> 2) & 15) == (r2 >> 4)) & ((c2 & 3) == (r2 & 3))
    )
    unsort_rows = jnp.where(unsort_rows, 1.0, 0.0).astype(BF16)

    def ag_copy(u, s, piece, to_n):
        ref = xbuf.at[u, piece]
        return remote(ref, ref, ag_s.at[u // 7], ag_r.at[u, s], w, to_n)

    def ag_half(u, s, piece, lower, to_n):
        ref = xbuf.at[u, piece, pl.ds(0 if lower else 32, 32)]
        return remote(ref, ref, ag_s.at[u // 7], ag_r.at[u, s], w, to_n)

    part = functools.partial

    def sends_a(u):
        return (
            (
                part(ag_copy, u, 0, n, dev_x),
                part(ag_copy, u, 1, n, dev_p),
                part(ag_copy, u, 1, n, dev_m),
            ),
            (part(ag_copy, u, 1, dev_x, dev_p), part(ag_copy, u, 1, dev_x, dev_m)),
            (part(ag_copy, u, 2, dev_m, dev_p), part(ag_copy, u, 2, at(yp, ox), dev_m)),
        )

    def sends_b(u):
        return (
            (
                part(ag_copy, u, 0, n, dev_p),
                part(ag_copy, u, 0, n, dev_m),
                part(ag_copy, u, 2, n, dev_x),
            ),
            (
                part(ag_half, u, 1, dev_m, True, dev_p),
                part(ag_half, u, 1, dev_p, False, dev_m),
                part(ag_copy, u, 2, dev_m, dev_x),
                part(ag_copy, u, 2, dev_p, dev_x),
            ),
            (part(ag_copy, u, 2, at(y2, xh), dev_x),),
        )

    def start_all(copies):
        for cp in copies:
            cp().start()

    def sort_stage(g):
        landed(a2abuf.at[g, pl.ds(0, WIDE - 1)], a2a_r.at[g])
        for arr in range(2):
            rows = dot(sort_rows, a2abuf[g, :, arr].reshape(256, qw)).astype(BF16)
            for q in range(4):
                xbuf[g * 4 + arr * 2 + q // 2, n, :, (q % 2) * qw : (q % 2 + 1) * qw] = rows[
                    q * ROWS : (q + 1) * ROWS
                ]

    def gg_copy(i):
        return remote(gbuf.at[n], gbuf.at[n], g_s.at[1], g_r.at[1], w, (n + i) % NARROW)

    pack(1)
    lag1, lag2, lag3 = GATHER_LAG

    @pl.loop(0, UNITS + lag3)
    def _(t):
        @pl.when(t < UNITS)
        def _():
            @pl.when(t % 4 == 0)
            def _():
                sort_stage(t // 4)

            @pl.when(gather_is_b(t))
            def _():
                start_all(sends_b(t)[0])

            @pl.when(jnp.logical_not(gather_is_b(t)))
            def _():
                start_all(sends_a(t)[0])

        @pl.when(t == 0)
        def _():
            post(1)

        @pl.when((t % 4 == 1) & (t // 4 + 2 < STAGES))
        def _():
            pack(t // 4 + 2)
            post(t // 4 + 2)

        @pl.when(t == 3)
        def _():
            landed(ga2a.at[pl.ds(0, WIDE - 1)], g_r.at[0])
            gbuf[n] = dot(sort_rows[0:ROWS], ga2a[...].reshape(256, 128)).astype(BF16)

            @pl.loop(1, NARROW)
            def _(i):
                gg_copy(i).start()

        @pl.when(t == lag3)
        def _():
            landed(gbuf.at[pl.ds(0, NARROW - 1)], g_r.at[1])
            here(wab.at[:, pl.ds(0, 2 * hid)], w_sem.at[0])
            here(wdn.at[:, pl.ds(0, hid)], w_sem.at[1])

        u1 = t - lag1

        @pl.when((u1 >= 0) & (u1 < UNITS))
        def _():
            @pl.when(gather_is_b(u1))
            def _():
                landed(xbuf.at[u1, pl.ds(0, 2)], ag_r.at[u1, 0])
                start_all(sends_b(u1)[1])

            @pl.when(jnp.logical_not(gather_is_b(u1)))
            def _():
                landed(xbuf.at[u1, 0], ag_r.at[u1, 0])
                start_all(sends_a(u1)[1])

        u2 = t - lag2

        @pl.when((u2 >= 0) & (u2 < UNITS))
        def _():
            @pl.when(gather_is_b(u2))
            def _():
                landed(xbuf.at[u2, 0], ag_r.at[u2, 1])
                start_all(sends_b(u2)[2])

            @pl.when(jnp.logical_not(gather_is_b(u2)))
            def _():
                landed(xbuf.at[u2, pl.ds(0, 4)], ag_r.at[u2, 1])
                start_all(sends_a(u2)[2])

        u3 = t - lag3

        @pl.when(u3 >= 0)
        def _():
            @pl.when(gather_is_b(u3))
            def _():
                landed(xbuf.at[u3, pl.ds(0, 4)], ag_r.at[u3, 2])

            @pl.when(jnp.logical_not(gather_is_b(u3)))
            def _():
                landed(xbuf.at[u3, pl.ds(0, 2)], ag_r.at[u3, 2])

            chunk = (u3 // 4) * 2 + u3 % 2
            is_cot = (u3 // 2) % 2 == 1

            @pl.when(is_cot)
            def _():
                acc_u[...] += dot_nt(xbuf[u3].reshape(512, cw), wdn[chunk])

            @pl.when(jnp.logical_not(is_cot))
            def _():
                acc_ab[...] += dot_nt(xbuf[u3].reshape(512, cw), wab[chunk])

    def hidden(r):
        span = slice(r * 128, (r + 1) * 128)
        g = gbuf[2 * r : 2 * r + 2].reshape(128, 128).astype(F32)
        g = jnp.concatenate([g, g], axis=1)
        a = acc_ab[span, 0:PAD]
        b = acc_ab[span, PAD : 2 * PAD]
        u = acc_u[span, :]
        s = jax.nn.sigmoid(a)
        act = a * s
        dh = g * u
        da = dh * b * s * (1.0 + a * (1.0 - s))
        du = dh * act
        h = act * b
        dd[span, 0:PAD] = da.astype(BF16)
        dd[span, PAD : 2 * PAD] = du.astype(BF16)
        acc_ab[span, 0:PAD] = h
        acc_u[span, :] = u * h

    for r in range(4):
        hidden(r)

    def turn():
        gp[4:8] = jnp.zeros((4, 128), F32)
        for r in range(4):
            span = slice(r * 128, (r + 1) * 128)
            dd_t[:, span] = dd[span, :].astype(F32).T.astype(BF16)
            hq_t[:, span] = acc_ab[span, 0:PAD].T.astype(BF16)
            gp[r : r + 1, :] = jnp.sum(acc_u[span, :].T, axis=0, keepdims=True)
        gpr[n] = gp[...]

        @pl.loop(1, NARROW)
        def _(i):
            gp_copy(i).start()

    def gp_copy(i):
        return remote(gp, gpr.at[n], g_s.at[2], g_r.at[2], w, (n + i) % NARROW)

    def gr_copy(i):
        e = (w + i) % WIDE
        return remote(gsum, gret.at[w], g_s.at[3], g_r.at[3], e, n)

    lo, hi = pl.ds(0, 32), pl.ds(32, 32)

    def c_copy(k, s, piece, slot, to_n):
        return remote(
            pbuf.at[k, piece], rb.at[k, slot], c_s.at[k // 7], c_r.at[k, s], w, to_n
        )

    def c_half(k, s, piece, slot, span, to_n):
        return remote(
            pbuf.at[k, piece, span], rb.at[k, slot, span], c_s.at[k // 7], c_r.at[k, s], w, to_n
        )

    def add_into(k, piece, slot, span=slice(None)):
        pbuf[k, piece, span] = (
            pbuf[k, piece, span].astype(F32) + rb[k, slot, span].astype(F32)
        ).astype(BF16)

    def red_a(k):
        return (
            (
                part(c_copy, k, 0, at(y2, 0), 0, dev_p),
                part(c_copy, k, 0, at(y2, 1), 1, dev_m),
                part(c_copy, k, 1, at(yp, 1), 3, dev_p),
                part(c_copy, k, 1, at(ym, 0), 4, dev_m),
            ),
            (
                part(c_copy, k, 1, at(yp, 0), 2, dev_p),
                part(c_copy, k, 1, at(ym, 1), 5, dev_m),
            ),
            (part(c_copy, k, 2, at(y, ox), 6, dev_x),),
        )

    def red_b(k):
        return (
            tuple(part(c_copy, k, 0, at(yy, ox), yy, dev_x) for yy in range(4)),
            (
                part(c_half, k, 1, at(y2, xh), 4, lo, dev_p),
                part(c_half, k, 1, at(y2, xh), 4, hi, dev_m),
                part(c_half, k, 2, at(yp, xh), 5, hi, dev_p),
                part(c_half, k, 2, at(ym, xh), 6, lo, dev_m),
            ),
            (
                part(c_half, k, 2, at(yp, xh), 5, lo, dev_p),
                part(c_half, k, 2, at(ym, xh), 6, hi, dev_m),
            ),
        )

    def ret_copy(g, i):
        to = (w + i) % WIDE
        return remote(
            retsend.at[g, to],
            ret_hbm.at[g, w],
            ret_s.at[g],
            ret_r.at[g],
            to,
            at(y, xh ^ swap(to, w)),
        )

    def own_copy(g):
        return pltpu.make_async_copy(retsend.at[g, w], ret_hbm.at[g, w], out_sem.at[1])

    def grad_copies(k):
        slot = k % 2
        return (
            pltpu.make_async_copy(
                stage_ab.at[slot, pl.ds(0, hid)], og_hbm.at[0, :, cols(k)], grad_sem.at[slot]
            ),
            pltpu.make_async_copy(
                stage_ab.at[slot, pl.ds(PAD, hid)], ou_hbm.at[0, :, cols(k)], grad_sem.at[slot]
            ),
            pltpu.make_async_copy(
                stage_d.at[slot, pl.ds(0, hid)], od_hbm.at[0, :, cols(k)], grad_sem.at[slot]
            ),
        )

    clag1, clag2, clag3 = REDUCE_LAG

    @pl.loop(0, CHUNKS + clag3)
    def _(t):
        @pl.when(t < CHUNKS)
        def _():
            pbuf[t] = dot(dd[...], wab[t]).astype(BF16).reshape(NARROW, ROWS, cw)

            @pl.when(reduce_is_b(t))
            def _():
                start_all(red_b(t)[0])

            @pl.when(jnp.logical_not(reduce_is_b(t)))
            def _():
                start_all(red_a(t)[0])

        k1 = t - clag1

        @pl.when((k1 >= 0) & (k1 < CHUNKS))
        def _():
            @pl.when(reduce_is_b(k1))
            def _():
                landed(rb.at[k1, pl.ds(0, 4)], c_r.at[k1, 0])
                for yy in (y2, yp, ym):
                    add_into(k1, at(yy, xh), yy)
                start_all(red_b(k1)[1])
                fin[k1] = pbuf[k1, n].astype(F32) + rb[k1, y].astype(F32)

            @pl.when(jnp.logical_not(reduce_is_b(k1)))
            def _():
                landed(rb.at[k1, pl.ds(0, 2)], c_r.at[k1, 0])
                add_into(k1, at(yp, 0), 0)
                add_into(k1, at(ym, 1), 1)
                start_all(red_a(k1)[1])

        k2 = t - clag2

        @pl.when((k2 >= 0) & (k2 < CHUNKS))
        def _():
            @pl.when(reduce_is_b(k2))
            def _():
                landed(rb.at[k2, 4], c_r.at[k2, 1])
                add_into(k2, at(yp, xh), 4, lo)
                add_into(k2, at(ym, xh), 4, hi)
                start_all(red_b(k2)[2])

            @pl.when(jnp.logical_not(reduce_is_b(k2)))
            def _():
                landed(rb.at[k2, pl.ds(2, 4)], c_r.at[k2, 1])
                other = at(y, ox)
                pbuf[k2, other] = (
                    pbuf[k2, other].astype(F32)
                    + rb[k2, 2 + ox].astype(F32)
                    + rb[k2, 4 + ox].astype(F32)
                ).astype(BF16)
                start_all(red_a(k2)[2])
                fin[k2] = (
                    pbuf[k2, n].astype(F32)
                    + rb[k2, 2 + xh].astype(F32)
                    + rb[k2, 4 + xh].astype(F32)
                )

        k3 = t - clag3

        @pl.when(k3 >= 0)
        def _():
            @pl.when(reduce_is_b(k3))
            def _():
                landed(rb.at[k3, pl.ds(5, 2)], c_r.at[k3, 2])
                rbuf[k3] = (
                    fin[k3] + rb[k3, 5].astype(F32) + rb[k3, 6].astype(F32)
                ).astype(BF16)

            @pl.when(jnp.logical_not(reduce_is_b(k3)))
            def _():
                landed(rb.at[k3, 6], c_r.at[k3, 2])
                rbuf[k3] = (fin[k3] + rb[k3, 6].astype(F32)).astype(BF16)

            @pl.when(k3 % 2 == 1)
            def _():
                g = k3 // 2
                rows = jnp.concatenate(
                    [
                        rbuf[2 * g + q // 2, :, (q % 2) * qw : (q % 2 + 1) * qw]
                        for q in range(4)
                    ],
                    axis=0,
                )
                retsend[g] = dot(unsort_rows, rows).astype(BF16).reshape(WIDE, 16, qw)

                @pl.loop(1, WIDE)
                def _(i):
                    ret_copy(g, i).start()

                own_copy(g).start()

        @pl.when(t == 1)
        def _():
            turn()

        kw = t - GRADS_LAG

        @pl.when((kw >= 0) & (kw < CHUNKS))
        def _():
            slot = kw % 2

            @pl.when(kw >= 2)
            def _():
                for cp in grad_copies(kw):
                    cp.wait()

            unit = (kw // 2) * 4 + kw % 2
            stage_ab[slot] = dot(dd_t[...], xbuf[unit].reshape(512, cw)).astype(BF16)

            @pl.loop(0, NARROW)
            def _(piece):
                g = gbuf[piece].astype(F32)
                g = jnp.concatenate([g] * (cw // 128), axis=1)
                qbuf[piece] = (g * xbuf[unit + 2, piece].astype(F32)).astype(BF16)

            stage_d[slot] = dot(hq_t[...], qbuf[...].reshape(512, cw)).astype(BF16)
            for cp in grad_copies(kw):
                cp.start()

        @pl.when(t == 6)
        def _():
            landed(gpr.at[pl.ds(0, NARROW - 1)], g_r.at[2])
            gsum[...] = jnp.sum(gpr[...], axis=0)
            gret[w] = gsum[...]

            @pl.loop(1, WIDE)
            def _(i):
                gr_copy(i).start()

    landed(gret.at[pl.ds(0, WIDE - 1)], g_r.at[3])

    row64 = iota((ROWS, WIDE), 0)
    spread = jnp.where((row64 >> 2) == iota((ROWS, WIDE), 1), 1.0, 0.0)
    line = gret[:, y, :]
    table = lax.dot_general(
        spread,
        line,
        (((1,), (0,)), ((), ())),
        precision=lax.Precision.HIGHEST,
        preferred_element_type=F32,
    )
    slot_row = iota((ROWS, 128), 0)
    turned = (((slot_row >> 3) & 1) ^ xl) & core
    lane = (xh ^ turned) * ROWS + w * CAP + (slot_row & 3)
    column = jnp.sum(
        jnp.where(iota((ROWS, 128), 1) == lane, table, 0.0), axis=1, keepdims=True
    )
    for k in range(8):
        match = target[k : k + 1, :] == slot_row
        gg_ref[k : k + 1, :] = jnp.sum(jnp.where(match, column, 0.0), axis=0, keepdims=True)

    sent(gsend.at[pl.ds(0, WIDE - 1)], g_s.at[0])
    sent(gbuf.at[pl.ds(0, NARROW - 1)], g_s.at[1])
    sent(gpr.at[pl.ds(0, NARROW - 1)], g_s.at[2])
    sent(gret.at[pl.ds(0, WIDE - 1)], g_s.at[3])
    for i in range(4):
        sent(xbuf.at[pl.ds(i * 7, 7), pl.ds(0, 7)], ag_s.at[i])
    for i in range(2):
        sent(pbuf.at[pl.ds(i * 7, 7), pl.ds(0, 7)], c_s.at[i])
    for k in range(CHUNKS - 2, CHUNKS):
        for cp in grad_copies(k):
            cp.wait()
    placet_copy.wait()

    @pl.loop(0, STAGES)
    def _(g):
        sent(sendbuf.at[g, pl.ds(0, WIDE - 1)], a2a_s.at[g])
        sent(retsend.at[g, pl.ds(0, WIDE - 1)], ret_s.at[g])
        landed(retsend.at[g, pl.ds(0, WIDE - 1)], ret_r.at[g])

    here(retsend.at[:, 0], out_sem.at[1])


def finish(
    placet_hbm,
    gg_ref,
    ret_hbm,
    og_in,
    ou_in,
    od_in,
    gt_hbm,
    gg_out,
    og_hbm,
    ou_hbm,
    od_hbm,
    placet,
    ret,
    gt,
    held,
    small_sem,
    in_sem,
    out_sem,
    gt_sem,
):
    qw = ret.shape[2]
    step = 32
    parts = held.shape[1] // step
    rows_in = (
        pltpu.make_async_copy(placet_hbm, placet, small_sem.at[0]),
        pltpu.make_async_copy(ret_hbm, ret, small_sem.at[1]),
    )
    loads, stores = [], []
    for i, (src, dst) in enumerate(((og_in, og_hbm), (ou_in, ou_hbm), (od_in, od_hbm))):
        for j in range(parts):
            span = pl.ds(j * step, step)
            here = held.at[i, span]
            loads.append(pltpu.make_async_copy(src.at[0, span], here, in_sem.at[i, j]))
            stores.append(pltpu.make_async_copy(here, dst.at[0, span], out_sem.at[i, j]))
    for cp in loads[:parts]:
        cp.start()
    for cp in rows_in:
        cp.start()
    for cp in loads[parts:]:
        cp.start()
    gg_out[...] = gg_ref[...]
    for load, store in zip(loads[:parts], stores[:parts]):
        load.wait()
        store.start()
    for cp in rows_in:
        cp.wait()
    homes = []
    for g in range(STAGES):
        home = dot(placet[...], ret[g]).astype(BF16)
        for q in range(4):
            gt[:, (g * 4 + q) * qw : (g * 4 + q + 1) * qw] = home[q * 128 : (q + 1) * 128]
        span = pl.ds(g * 4 * qw, 4 * qw)
        homes.append(pltpu.make_async_copy(gt.at[:, span], gt_hbm.at[:, span], gt_sem.at[g]))
        homes[-1].start()
        for k in range(parts + 2 * g, parts + 2 * g + 2):
            loads[k].wait()
            stores[k].start()
    for cp in stores + homes:
        cp.wait()


def per_device(tokens, grad_out, gates, expert_ids, slots, w_gate, w_up, w_down):
    width = tokens.shape[1]
    cw = width // CHUNKS
    any_spec = pl.BlockSpec(memory_space=pl.ANY)
    vmem_spec = pl.BlockSpec(memory_space=pltpu.VMEM)
    vm = pltpu.VMEM
    dma = pltpu.SemaphoreType.DMA
    sds = jax.ShapeDtypeStruct
    og, ou, od, placet, ret, gg = pl.pallas_call(
        kernel,
        out_shape=(
            sds(w_gate.shape, BF16),
            sds(w_up.shape, BF16),
            sds(w_down.shape, BF16),
            sds((512, 256), BF16),
            sds((STAGES, WIDE, 16, cw // 2), BF16),
            sds((8, 128), F32),
        ),
        in_specs=[vmem_spec] * 3 + [any_spec] * 5,
        out_specs=(any_spec,) * 5 + (vmem_spec,),
        scratch_shapes=[
            vm((256, 512), BF16),
            vm((512, 256), BF16),
            vm((STAGES, 2, 128, 2 * cw), BF16),
            vm((STAGES, WIDE, 2, 16, cw // 2), BF16),
            vm((STAGES, WIDE, 2, 16, cw // 2), BF16),
            vm((UNITS, NARROW, ROWS, cw), BF16),
            vm((CHUNKS, 2 * PAD, cw), BF16),
            vm((CHUNKS, PAD, cw), BF16),
            vm((512, 2 * PAD), F32),
            vm((512, PAD), F32),
            vm((WIDE, 16, 128), BF16),
            vm((WIDE, 16, 128), BF16),
            vm((NARROW, ROWS, 128), BF16),
            vm((512, 2 * PAD), BF16),
            vm((2 * PAD, 512), BF16),
            vm((PAD, 512), BF16),
            vm((CHUNKS, NARROW, ROWS, cw), BF16),
            vm((CHUNKS, 7, ROWS, cw), BF16),
            vm((CHUNKS, ROWS, cw), F32),
            vm((CHUNKS, ROWS, cw), BF16),
            vm((STAGES, WIDE, 16, cw // 2), BF16),
            vm((NARROW, ROWS, cw), BF16),
            vm((2, 2 * PAD, cw), BF16),
            vm((2, PAD, cw), BF16),
            vm((8, 128), F32),
            vm((NARROW, 8, 128), F32),
            vm((8, 128), F32),
            vm((WIDE, 8, 128), F32),
            dma((STAGES,)),
            dma((2,)),
            dma((STAGES,)),
            dma((STAGES,)),
            dma((4,)),
            dma((4,)),
            dma((4,)),
            dma((UNITS, 3)),
            dma((2,)),
            dma((CHUNKS, 3)),
            dma((STAGES,)),
            dma((STAGES,)),
            dma((2,)),
            dma((2,)),
        ],
        compiler_params=pltpu.CompilerParams(
            collective_id=0, has_side_effects=True, vmem_limit_bytes=63 * 2**20
        ),
        name="routed_backward",
    )(
        expert_ids.T,
        slots.T,
        gates.T,
        tokens,
        grad_out,
        w_gate,
        w_up,
        w_down,
    )
    ret = ret.reshape(STAGES, 256, cw // 2)
    gt, gg, og, ou, od = pl.pallas_call(
        finish,
        in_specs=[any_spec, vmem_spec] + [any_spec] * 4,
        out_specs=(any_spec, vmem_spec) + (any_spec,) * 3,
        out_shape=(
            sds(tokens.shape, BF16),
            sds((8, 128), F32),
            sds(w_gate.shape, BF16),
            sds(w_up.shape, BF16),
            sds(w_down.shape, BF16),
        ),
        scratch_shapes=[
            vm((512, 256), BF16),
            vm((STAGES, 256, cw // 2), BF16),
            vm(tokens.shape, BF16),
            vm((3,) + w_gate.shape[1:], BF16),
            dma((2,)),
            dma((3, 7)),
            dma((3, 7)),
            dma((STAGES,)),
        ],
        compiler_params=pltpu.CompilerParams(vmem_limit_bytes=62 * 2**20),
        name="finish",
    )(placet, gg, ret, og, ou, od)
    return (gt, gg.T, og, ou, od)


def solution(mesh):
    rows = P(("wide", "narrow"), None)
    weights = P("wide", "narrow", None)
    return jax.shard_map(
        per_device,
        mesh=mesh,
        in_specs=(rows,) * 5 + (weights,) * 3,
        out_specs=(rows, rows, weights, weights, weights),
        check_vma=False,
    )
```

```python
import functools

import jax
import jax.numpy as jnp
from jax import lax
from jax.experimental import pallas as pl
from jax.experimental.pallas import tpu as pltpu
from jax.sharding import PartitionSpec as P

CAP = 4
WIDE = 16
NARROW = 8
ROWS = WIDE * CAP
STAGES = 7
CHUNKS = 2 * STAGES
UNITS = 2 * CHUNKS
GATHER_LAG = (2, 4, 6)
REDUCE_LAG = (4, 8, 12)
GRADS_LAG = 4
PAD = 256
MESH = pl.DeviceIdType.MESH
F32 = jnp.float32
BF16 = jnp.bfloat16


def dot(left, right):
    return jnp.dot(left, right, preferred_element_type=F32)


def dot_nt(left, right):
    return lax.dot_general(left, right, (((1,), (1,)), ((), ())), preferred_element_type=F32)


def iota(shape, dim):
    return lax.broadcasted_iota(jnp.int32, shape, dim)


def gather_is_b(unit):
    return (unit * 11) % 28 < 11


def reduce_is_b(chunk):
    return (chunk * 5 + 9) % 14 < 5


def kernel(
    ids_ref,
    slots_ref,
    gates_ref,
    tok_hbm,
    cot_hbm,
    wg_hbm,
    wu_hbm,
    wd_hbm,
    og_hbm,
    ou_hbm,
    od_hbm,
    placet_hbm,
    ret_hbm,
    gg_hbm,
    place,
    place_t,
    tokbuf,
    sendbuf,
    a2abuf,
    xbuf,
    wab,
    wdn,
    acc_ab,
    acc_u,
    gsend,
    ga2a,
    gbuf,
    dd,
    dd_t,
    hq_t,
    pbuf,
    rb,
    fin,
    rbuf,
    retsend,
    qbuf,
    stage_ab,
    stage_d,
    gp,
    gpr,
    gsum,
    gret,
    gg_ref,
    tok_sem,
    w_sem,
    a2a_s,
    a2a_r,
    g_s,
    g_r,
    ag_s,
    ag_r,
    c_s,
    c_r,
    ret_s,
    ret_r,
    grad_sem,
    out_sem,
):
    w = lax.axis_index("wide")
    n = lax.axis_index("narrow")
    y, xh = n // 2, n % 2
    yp, ym, y2 = (y + 1) % 4, (y + 3) % 4, (y + 2) % 4
    ox = 1 - xh
    cw = xbuf.shape[3]
    qw = cw // 2
    sw = 2 * cw
    hid = wg_hbm.shape[1]

    def at(yy, xx):
        return yy * 2 + xx

    xl, core = (w // 2) % 2, w % 2

    def swap(source, expert):
        return (((source // 2) % 2) ^ ((expert // 2) % 2)) & (source % 2)

    dev_p, dev_m, dev_x = at(yp, xh), at(ym, xh), at(y, ox)

    def cols(chunk):
        return pl.ds(pl.multiple_of(chunk * cw, 128), cw)

    def remote(src, dst, ss, rs, to_w, to_n):
        return pltpu.make_async_remote_copy(
            src_ref=src,
            dst_ref=dst,
            send_sem=ss,
            recv_sem=rs,
            device_id=(to_w, to_n),
            device_id_type=MESH,
        )

    barrier = pltpu.get_barrier_semaphore()

    @pl.loop(1, WIDE)
    def _(i):
        pl.semaphore_signal(barrier, inc=1, device_id=((w + i) % WIDE, n), device_id_type=MESH)

    @pl.loop(0, WIDE)
    def _(i):
        pl.semaphore_signal(barrier, inc=1, device_id=(i, at(y, ox)), device_id_type=MESH)

    @pl.loop(1, 4)
    def _(i):
        for xx in range(2):
            pl.semaphore_signal(
                barrier, inc=1, device_id=(w, at((y + i) % 4, xx)), device_id_type=MESH
            )

    def tok_copy(g, arr):
        src = tok_hbm if arr == 0 else cot_hbm
        span = pl.ds(pl.multiple_of(g * sw, 128), sw)
        return pltpu.make_async_copy(src.at[:, span], tokbuf.at[g, arr], tok_sem.at[g])

    @pl.loop(0, STAGES)
    def _(g):
        for arr in range(2):
            tok_copy(g, arr).start()

    def w_copies(chunk):
        return (
            pltpu.make_async_copy(
                wg_hbm.at[0, :, cols(chunk)], wab.at[chunk, pl.ds(0, hid)], w_sem.at[0]
            ),
            pltpu.make_async_copy(
                wu_hbm.at[0, :, cols(chunk)], wab.at[chunk, pl.ds(PAD, hid)], w_sem.at[0]
            ),
            pltpu.make_async_copy(
                wd_hbm.at[0, :, cols(chunk)], wdn.at[chunk, pl.ds(0, hid)], w_sem.at[1]
            ),
        )

    def landed(ref, sem):
        remote(ref, ref, sem, sem, w, n ^ 1).wait_recv()

    def sent(ref, sem):
        remote(ref, ref, sem, sem, w, n ^ 1).wait_send()

    def here(ref, sem):
        pltpu.make_async_copy(ref, ref, sem).wait()

    kept = (ids_ref[...] < WIDE) & (slots_ref[...] < CAP)
    target = jnp.where(kept, ids_ref[...] * CAP + slots_ref[...], ROWS)
    row = iota((256, 128), 0)
    code = (row >> 4) * CAP + (row & 3)
    gates = gates_ref[...].astype(F32)
    hit = jnp.zeros((256, 128), F32)
    weight = jnp.zeros((256, 128), F32)
    for k in range(8):
        match = target[k : k + 1, :] == code
        hit = hit + jnp.where(match, 1.0, 0.0)
        weight = weight + jnp.where(match, gates[k : k + 1, :], 0.0)
    for q in range(4):
        part = jnp.where(((row >> 2) & 3) == q, hit, 0.0)
        place[:, q * 128 : (q + 1) * 128] = part.astype(BF16)
        place_t[q * 128 : (q + 1) * 128, :] = part.T.astype(BF16)
    gsend[...] = (
        dot(weight.astype(BF16), jnp.ones((128, 128), BF16)).astype(BF16).reshape(WIDE, 16, 128)
    )

    def a2a_copy(g, i):
        e = (w + i) % WIDE
        return remote(
            sendbuf.at[g, e],
            a2abuf.at[g, w],
            a2a_s.at[g],
            a2a_r.at[g],
            e,
            at(y, xh ^ swap(w, e)),
        )

    def ga_copy(i):
        e = (w + i) % WIDE
        return remote(gsend.at[e], ga2a.at[w], g_s.at[0], g_r.at[0], e, at(y, xh ^ swap(w, e)))

    def pack(g):
        here(tokbuf.at[g], tok_sem.at[g])
        for arr in range(2):
            slab = jnp.concatenate(
                [tokbuf[g, arr, :, q * qw : (q + 1) * qw] for q in range(4)], axis=0
            )
            sendbuf[g, :, arr] = dot(place[...], slab).astype(BF16).reshape(WIDE, 16, qw)

    def post(g):
        @pl.loop(1, WIDE)
        def _(i):
            a2a_copy(g, i).start()

        a2abuf[g, w] = sendbuf[g, w]

    pack(0)
    pl.semaphore_wait(barrier, 2 * WIDE - 1 + NARROW - 2)
    post(0)

    @pl.loop(1, WIDE)
    def _(i):
        ga_copy(i).start()

    ga2a[w] = gsend[w]

    @pl.loop(0, CHUNKS)
    def _(chunk):
        for cp in w_copies(chunk):
            cp.start()
        wab[chunk, hid:PAD] = jnp.zeros((PAD - hid, cw), BF16)
        wab[chunk, PAD + hid :] = jnp.zeros((PAD - hid, cw), BF16)
        wdn[chunk, hid:] = jnp.zeros((PAD - hid, cw), BF16)

    placet_copy = pltpu.make_async_copy(place_t, placet_hbm, out_sem.at[0])
    placet_copy.start()
    acc_ab[...] = jnp.zeros_like(acc_ab)
    acc_u[...] = jnp.zeros_like(acc_u)

    r2, c2 = iota((256, 256), 0), iota((256, 256), 1)
    sort_rows = (
        ((r2 >> 6) == ((c2 >> 2) & 3)) & (((r2 >> 2) & 15) == (c2 >> 4)) & ((r2 & 3) == (c2 & 3))
    )
    sort_rows = jnp.where(sort_rows, 1.0, 0.0).astype(BF16)
    unsort_rows = (
        ((c2 >> 6) == ((r2 >> 2) & 3)) & (((c2 >> 2) & 15) == (r2 >> 4)) & ((c2 & 3) == (r2 & 3))
    )
    unsort_rows = jnp.where(unsort_rows, 1.0, 0.0).astype(BF16)

    def ag_copy(u, s, piece, to_n):
        ref = xbuf.at[u, piece]
        return remote(ref, ref, ag_s.at[u // 7], ag_r.at[u, s], w, to_n)

    def ag_half(u, s, piece, lower, to_n):
        ref = xbuf.at[u, piece, pl.ds(0 if lower else 32, 32)]
        return remote(ref, ref, ag_s.at[u // 7], ag_r.at[u, s], w, to_n)

    part = functools.partial

    def sends_a(u):
        return (
            (
                part(ag_copy, u, 0, n, dev_x),
                part(ag_copy, u, 1, n, dev_p),
                part(ag_copy, u, 1, n, dev_m),
            ),
            (part(ag_copy, u, 1, dev_x, dev_p), part(ag_copy, u, 1, dev_x, dev_m)),
            (part(ag_copy, u, 2, dev_m, dev_p), part(ag_copy, u, 2, at(yp, ox), dev_m)),
        )

    def sends_b(u):
        return (
            (
                part(ag_copy, u, 0, n, dev_p),
                part(ag_copy, u, 0, n, dev_m),
                part(ag_copy, u, 2, n, dev_x),
            ),
            (
                part(ag_half, u, 1, dev_m, True, dev_p),
                part(ag_half, u, 1, dev_p, False, dev_m),
                part(ag_copy, u, 2, dev_m, dev_x),
                part(ag_copy, u, 2, dev_p, dev_x),
            ),
            (part(ag_copy, u, 2, at(y2, xh), dev_x),),
        )

    def start_all(copies):
        for cp in copies:
            cp().start()

    def sort_stage(g):
        landed(a2abuf.at[g, pl.ds(0, WIDE - 1)], a2a_r.at[g])
        for arr in range(2):
            rows = dot(sort_rows, a2abuf[g, :, arr].reshape(256, qw)).astype(BF16)
            for q in range(4):
                xbuf[g * 4 + arr * 2 + q // 2, n, :, (q % 2) * qw : (q % 2 + 1) * qw] = rows[
                    q * ROWS : (q + 1) * ROWS
                ]

    def gg_copy(i):
        return remote(gbuf.at[n], gbuf.at[n], g_s.at[1], g_r.at[1], w, (n + i) % NARROW)

    pack(1)
    lag1, lag2, lag3 = GATHER_LAG

    @pl.loop(0, UNITS + lag3)
    def _(t):
        @pl.when(t < UNITS)
        def _():
            @pl.when(t % 4 == 0)
            def _():
                sort_stage(t // 4)

            @pl.when(gather_is_b(t))
            def _():
                start_all(sends_b(t)[0])

            @pl.when(jnp.logical_not(gather_is_b(t)))
            def _():
                start_all(sends_a(t)[0])

        @pl.when(t == 0)
        def _():
            post(1)

        @pl.when((t % 4 == 1) & (t // 4 + 2 < STAGES))
        def _():
            pack(t // 4 + 2)
            post(t // 4 + 2)

        @pl.when(t == 3)
        def _():
            landed(ga2a.at[pl.ds(0, WIDE - 1)], g_r.at[0])
            gbuf[n] = dot(sort_rows[0:ROWS], ga2a[...].reshape(256, 128)).astype(BF16)

            @pl.loop(1, NARROW)
            def _(i):
                gg_copy(i).start()

        @pl.when(t == lag3)
        def _():
            landed(gbuf.at[pl.ds(0, NARROW - 1)], g_r.at[1])
            here(wab.at[:, pl.ds(0, 2 * hid)], w_sem.at[0])
            here(wdn.at[:, pl.ds(0, hid)], w_sem.at[1])

        u1 = t - lag1

        @pl.when((u1 >= 0) & (u1 < UNITS))
        def _():
            @pl.when(gather_is_b(u1))
            def _():
                landed(xbuf.at[u1, pl.ds(0, 2)], ag_r.at[u1, 0])
                start_all(sends_b(u1)[1])

            @pl.when(jnp.logical_not(gather_is_b(u1)))
            def _():
                landed(xbuf.at[u1, 0], ag_r.at[u1, 0])
                start_all(sends_a(u1)[1])

        u2 = t - lag2

        @pl.when((u2 >= 0) & (u2 < UNITS))
        def _():
            @pl.when(gather_is_b(u2))
            def _():
                landed(xbuf.at[u2, 0], ag_r.at[u2, 1])
                start_all(sends_b(u2)[2])

            @pl.when(jnp.logical_not(gather_is_b(u2)))
            def _():
                landed(xbuf.at[u2, pl.ds(0, 4)], ag_r.at[u2, 1])
                start_all(sends_a(u2)[2])

        u3 = t - lag3

        @pl.when(u3 >= 0)
        def _():
            @pl.when(gather_is_b(u3))
            def _():
                landed(xbuf.at[u3, pl.ds(0, 4)], ag_r.at[u3, 2])

            @pl.when(jnp.logical_not(gather_is_b(u3)))
            def _():
                landed(xbuf.at[u3, pl.ds(0, 2)], ag_r.at[u3, 2])

            chunk = (u3 // 4) * 2 + u3 % 2
            is_cot = (u3 // 2) % 2 == 1

            @pl.when(is_cot)
            def _():
                acc_u[...] += dot_nt(xbuf[u3].reshape(512, cw), wdn[chunk])

            @pl.when(jnp.logical_not(is_cot))
            def _():
                acc_ab[...] += dot_nt(xbuf[u3].reshape(512, cw), wab[chunk])

    def hidden(r):
        span = slice(r * 128, (r + 1) * 128)
        g = gbuf[2 * r : 2 * r + 2].reshape(128, 128).astype(F32)
        g = jnp.concatenate([g, g], axis=1)
        a = acc_ab[span, 0:PAD]
        b = acc_ab[span, PAD : 2 * PAD]
        u = acc_u[span, :]
        s = jax.nn.sigmoid(a)
        act = a * s
        dh = g * u
        da = dh * b * s * (1.0 + a * (1.0 - s))
        du = dh * act
        h = act * b
        dd[span, 0:PAD] = da.astype(BF16)
        dd[span, PAD : 2 * PAD] = du.astype(BF16)
        acc_ab[span, 0:PAD] = h
        acc_u[span, :] = u * h

    for r in range(4):
        hidden(r)

    def turn():
        gp[4:8] = jnp.zeros((4, 128), F32)
        for r in range(4):
            span = slice(r * 128, (r + 1) * 128)
            dd_t[:, span] = dd[span, :].astype(F32).T.astype(BF16)
            hq_t[:, span] = acc_ab[span, 0:PAD].T.astype(BF16)
            gp[r : r + 1, :] = jnp.sum(acc_u[span, :].T, axis=0, keepdims=True)
        gpr[n] = gp[...]

        @pl.loop(1, NARROW)
        def _(i):
            gp_copy(i).start()

    def gp_copy(i):
        return remote(gp, gpr.at[n], g_s.at[2], g_r.at[2], w, (n + i) % NARROW)

    def gr_copy(i):
        e = (w + i) % WIDE
        return remote(gsum, gret.at[w], g_s.at[3], g_r.at[3], e, n)

    lo, hi = pl.ds(0, 32), pl.ds(32, 32)

    def c_copy(k, s, piece, slot, to_n):
        return remote(
            pbuf.at[k, piece], rb.at[k, slot], c_s.at[k // 7], c_r.at[k, s], w, to_n
        )

    def c_half(k, s, piece, slot, span, to_n):
        return remote(
            pbuf.at[k, piece, span], rb.at[k, slot, span], c_s.at[k // 7], c_r.at[k, s], w, to_n
        )

    def add_into(k, piece, slot, span=slice(None)):
        pbuf[k, piece, span] = (
            pbuf[k, piece, span].astype(F32) + rb[k, slot, span].astype(F32)
        ).astype(BF16)

    def red_a(k):
        return (
            (
                part(c_copy, k, 0, at(y2, 0), 0, dev_p),
                part(c_copy, k, 0, at(y2, 1), 1, dev_m),
                part(c_copy, k, 1, at(yp, 1), 3, dev_p),
                part(c_copy, k, 1, at(ym, 0), 4, dev_m),
            ),
            (
                part(c_copy, k, 1, at(yp, 0), 2, dev_p),
                part(c_copy, k, 1, at(ym, 1), 5, dev_m),
            ),
            (part(c_copy, k, 2, at(y, ox), 6, dev_x),),
        )

    def red_b(k):
        return (
            tuple(part(c_copy, k, 0, at(yy, ox), yy, dev_x) for yy in range(4)),
            (
                part(c_half, k, 1, at(y2, xh), 4, lo, dev_p),
                part(c_half, k, 1, at(y2, xh), 4, hi, dev_m),
                part(c_half, k, 2, at(yp, xh), 5, hi, dev_p),
                part(c_half, k, 2, at(ym, xh), 6, lo, dev_m),
            ),
            (
                part(c_half, k, 2, at(yp, xh), 5, lo, dev_p),
                part(c_half, k, 2, at(ym, xh), 6, hi, dev_m),
            ),
        )

    def ret_copy(g, i):
        to = (w + i) % WIDE
        return remote(
            retsend.at[g, to],
            ret_hbm.at[g, w],
            ret_s.at[g],
            ret_r.at[g],
            to,
            at(y, xh ^ swap(to, w)),
        )

    def own_copy(g):
        return pltpu.make_async_copy(retsend.at[g, w], ret_hbm.at[g, w], out_sem.at[1])

    def grad_copies(k):
        slot = k % 2
        return (
            pltpu.make_async_copy(
                stage_ab.at[slot, pl.ds(0, hid)], og_hbm.at[0, :, cols(k)], grad_sem.at[slot]
            ),
            pltpu.make_async_copy(
                stage_ab.at[slot, pl.ds(PAD, hid)], ou_hbm.at[0, :, cols(k)], grad_sem.at[slot]
            ),
            pltpu.make_async_copy(
                stage_d.at[slot, pl.ds(0, hid)], od_hbm.at[0, :, cols(k)], grad_sem.at[slot]
            ),
        )

    gg_copy_out = pltpu.make_async_copy(gg_ref, gg_hbm, out_sem.at[2])

    def router():
        landed(gret.at[pl.ds(0, WIDE - 1)], g_r.at[3])

        row64 = iota((ROWS, WIDE), 0)
        spread = jnp.where((row64 >> 2) == iota((ROWS, WIDE), 1), 1.0, 0.0)
        line = gret[:, y, :]
        table = lax.dot_general(
            spread,
            line,
            (((1,), (0,)), ((), ())),
            precision=lax.Precision.HIGHEST,
            preferred_element_type=F32,
        )
        slot_row = iota((ROWS, 128), 0)
        turned = (((slot_row >> 3) & 1) ^ xl) & core
        lane = (xh ^ turned) * ROWS + w * CAP + (slot_row & 3)
        column = jnp.sum(
            jnp.where(iota((ROWS, 128), 1) == lane, table, 0.0), axis=1, keepdims=True
        )
        for k in range(8):
            match = target[k : k + 1, :] == slot_row
            gg_ref[k : k + 1, :] = jnp.sum(jnp.where(match, column, 0.0), axis=0, keepdims=True)
        gg_copy_out.start()

    clag1, clag2, clag3 = REDUCE_LAG

    @pl.loop(0, CHUNKS + clag3)
    def _(t):
        @pl.when(t < CHUNKS)
        def _():
            pbuf[t] = dot(dd[...], wab[t]).astype(BF16).reshape(NARROW, ROWS, cw)

            @pl.when(reduce_is_b(t))
            def _():
                start_all(red_b(t)[0])

            @pl.when(jnp.logical_not(reduce_is_b(t)))
            def _():
                start_all(red_a(t)[0])

        k1 = t - clag1

        @pl.when((k1 >= 0) & (k1 < CHUNKS))
        def _():
            @pl.when(reduce_is_b(k1))
            def _():
                landed(rb.at[k1, pl.ds(0, 4)], c_r.at[k1, 0])
                for yy in (y2, yp, ym):
                    add_into(k1, at(yy, xh), yy)
                start_all(red_b(k1)[1])
                fin[k1] = pbuf[k1, n].astype(F32) + rb[k1, y].astype(F32)

            @pl.when(jnp.logical_not(reduce_is_b(k1)))
            def _():
                landed(rb.at[k1, pl.ds(0, 2)], c_r.at[k1, 0])
                add_into(k1, at(yp, 0), 0)
                add_into(k1, at(ym, 1), 1)
                start_all(red_a(k1)[1])

        k2 = t - clag2

        @pl.when((k2 >= 0) & (k2 < CHUNKS))
        def _():
            @pl.when(reduce_is_b(k2))
            def _():
                landed(rb.at[k2, 4], c_r.at[k2, 1])
                add_into(k2, at(yp, xh), 4, lo)
                add_into(k2, at(ym, xh), 4, hi)
                start_all(red_b(k2)[2])

            @pl.when(jnp.logical_not(reduce_is_b(k2)))
            def _():
                landed(rb.at[k2, pl.ds(2, 4)], c_r.at[k2, 1])
                other = at(y, ox)
                pbuf[k2, other] = (
                    pbuf[k2, other].astype(F32)
                    + rb[k2, 2 + ox].astype(F32)
                    + rb[k2, 4 + ox].astype(F32)
                ).astype(BF16)
                start_all(red_a(k2)[2])
                fin[k2] = (
                    pbuf[k2, n].astype(F32)
                    + rb[k2, 2 + xh].astype(F32)
                    + rb[k2, 4 + xh].astype(F32)
                )

        k3 = t - clag3

        @pl.when(k3 >= 0)
        def _():
            @pl.when(reduce_is_b(k3))
            def _():
                landed(rb.at[k3, pl.ds(5, 2)], c_r.at[k3, 2])
                rbuf[k3] = (
                    fin[k3] + rb[k3, 5].astype(F32) + rb[k3, 6].astype(F32)
                ).astype(BF16)

            @pl.when(jnp.logical_not(reduce_is_b(k3)))
            def _():
                landed(rb.at[k3, 6], c_r.at[k3, 2])
                rbuf[k3] = (fin[k3] + rb[k3, 6].astype(F32)).astype(BF16)

            @pl.when(k3 % 2 == 1)
            def _():
                g = k3 // 2
                rows = jnp.concatenate(
                    [
                        rbuf[2 * g + q // 2, :, (q % 2) * qw : (q % 2 + 1) * qw]
                        for q in range(4)
                    ],
                    axis=0,
                )
                retsend[g] = dot(unsort_rows, rows).astype(BF16).reshape(WIDE, 16, qw)

                @pl.loop(1, WIDE)
                def _(i):
                    ret_copy(g, i).start()

                own_copy(g).start()

        @pl.when(t == 3)
        def _():
            turn()

        @pl.when(t == CHUNKS + 4)
        def _():
            router()

        kw = t - GRADS_LAG

        @pl.when((kw >= 0) & (kw < CHUNKS))
        def _():
            slot = kw % 2

            @pl.when(kw >= 2)
            def _():
                for cp in grad_copies(kw):
                    cp.wait()

            unit = (kw // 2) * 4 + kw % 2
            stage_ab[slot] = dot(dd_t[...], xbuf[unit].reshape(512, cw)).astype(BF16)

            @pl.loop(0, NARROW)
            def _(piece):
                g = gbuf[piece].astype(F32)
                g = jnp.concatenate([g] * (cw // 128), axis=1)
                qbuf[piece] = (g * xbuf[unit + 2, piece].astype(F32)).astype(BF16)

            stage_d[slot] = dot(hq_t[...], qbuf[...].reshape(512, cw)).astype(BF16)
            for cp in grad_copies(kw):
                cp.start()

        @pl.when(t == 9)
        def _():
            landed(gpr.at[pl.ds(0, NARROW - 1)], g_r.at[2])
            gsum[...] = jnp.sum(gpr[...], axis=0)
            gret[w] = gsum[...]

            @pl.loop(1, WIDE)
            def _(i):
                gr_copy(i).start()

    sent(gsend.at[pl.ds(0, WIDE - 1)], g_s.at[0])
    sent(gbuf.at[pl.ds(0, NARROW - 1)], g_s.at[1])
    sent(gpr.at[pl.ds(0, NARROW - 1)], g_s.at[2])
    sent(gret.at[pl.ds(0, WIDE - 1)], g_s.at[3])
    for i in range(4):
        sent(xbuf.at[pl.ds(i * 7, 7), pl.ds(0, 7)], ag_s.at[i])
    for i in range(2):
        sent(pbuf.at[pl.ds(i * 7, 7), pl.ds(0, 7)], c_s.at[i])
    for k in range(CHUNKS - 2, CHUNKS):
        for cp in grad_copies(k):
            cp.wait()
    placet_copy.wait()
    gg_copy_out.wait()

    @pl.loop(0, STAGES)
    def _(g):
        sent(sendbuf.at[g, pl.ds(0, WIDE - 1)], a2a_s.at[g])
        sent(retsend.at[g, pl.ds(0, WIDE - 1)], ret_s.at[g])
        landed(retsend.at[g, pl.ds(0, WIDE - 1)], ret_r.at[g])

    here(retsend.at[:, 0], out_sem.at[1])


def finish(
    placet_hbm,
    gg_in,
    ret_hbm,
    og_in,
    ou_in,
    od_in,
    gt_hbm,
    gg_out,
    og_hbm,
    ou_hbm,
    od_hbm,
    gg,
    placet,
    ret,
    gt,
    held,
    small_sem,
    in_sem,
    out_sem,
    gt_sem,
):
    qw = ret.shape[2]
    step = 32
    parts = held.shape[1] // step
    rows_in = (
        pltpu.make_async_copy(placet_hbm, placet, small_sem.at[0]),
        pltpu.make_async_copy(ret_hbm, ret, small_sem.at[1]),
        pltpu.make_async_copy(gg_in, gg, small_sem.at[2]),
    )
    loads, stores = [], []
    for i, (src, dst) in enumerate(((og_in, og_hbm), (ou_in, ou_hbm), (od_in, od_hbm))):
        for j in range(parts):
            span = pl.ds(j * step, step)
            here = held.at[i, span]
            loads.append(pltpu.make_async_copy(src.at[0, span], here, in_sem.at[i, j]))
            stores.append(pltpu.make_async_copy(here, dst.at[0, span], out_sem.at[i, j]))
    for cp in loads[:parts]:
        cp.start()
    for cp in rows_in:
        cp.start()
    for cp in loads[parts:]:
        cp.start()
    for load, store in zip(loads[:parts], stores[:parts]):
        load.wait()
        store.start()
    for cp in rows_in:
        cp.wait()
    homes = [pltpu.make_async_copy(gg, gg_out, gt_sem.at[STAGES])]
    homes[0].start()
    for g in range(STAGES):
        home = dot(placet[...], ret[g]).astype(BF16)
        for q in range(4):
            gt[:, (g * 4 + q) * qw : (g * 4 + q + 1) * qw] = home[q * 128 : (q + 1) * 128]
        span = pl.ds(g * 4 * qw, 4 * qw)
        homes.append(pltpu.make_async_copy(gt.at[:, span], gt_hbm.at[:, span], gt_sem.at[g]))
        homes[-1].start()
        for k in range(parts + 2 * g, parts + 2 * g + 2):
            loads[k].wait()
            stores[k].start()
    for cp in stores + homes:
        cp.wait()


def per_device(tokens, grad_out, gates, expert_ids, slots, w_gate, w_up, w_down):
    width = tokens.shape[1]
    cw = width // CHUNKS
    any_spec = pl.BlockSpec(memory_space=pl.ANY)
    vmem_spec = pl.BlockSpec(memory_space=pltpu.VMEM)
    vm = pltpu.VMEM
    dma = pltpu.SemaphoreType.DMA
    sds = jax.ShapeDtypeStruct
    og, ou, od, placet, ret, gg = pl.pallas_call(
        kernel,
        out_shape=(
            sds(w_gate.shape, BF16),
            sds(w_up.shape, BF16),
            sds(w_down.shape, BF16),
            sds((512, 256), BF16),
            sds((STAGES, WIDE, 16, cw // 2), BF16),
            sds((8, 128), F32),
        ),
        in_specs=[vmem_spec] * 3 + [any_spec] * 5,
        out_specs=(any_spec,) * 6,
        scratch_shapes=[
            vm((256, 512), BF16),
            vm((512, 256), BF16),
            vm((STAGES, 2, 128, 2 * cw), BF16),
            vm((STAGES, WIDE, 2, 16, cw // 2), BF16),
            vm((STAGES, WIDE, 2, 16, cw // 2), BF16),
            vm((UNITS, NARROW, ROWS, cw), BF16),
            vm((CHUNKS, 2 * PAD, cw), BF16),
            vm((CHUNKS, PAD, cw), BF16),
            vm((512, 2 * PAD), F32),
            vm((512, PAD), F32),
            vm((WIDE, 16, 128), BF16),
            vm((WIDE, 16, 128), BF16),
            vm((NARROW, ROWS, 128), BF16),
            vm((512, 2 * PAD), BF16),
            vm((2 * PAD, 512), BF16),
            vm((PAD, 512), BF16),
            vm((CHUNKS, NARROW, ROWS, cw), BF16),
            vm((CHUNKS, 7, ROWS, cw), BF16),
            vm((CHUNKS, ROWS, cw), F32),
            vm((CHUNKS, ROWS, cw), BF16),
            vm((STAGES, WIDE, 16, cw // 2), BF16),
            vm((NARROW, ROWS, cw), BF16),
            vm((2, 2 * PAD, cw), BF16),
            vm((2, PAD, cw), BF16),
            vm((8, 128), F32),
            vm((NARROW, 8, 128), F32),
            vm((8, 128), F32),
            vm((WIDE, 8, 128), F32),
            vm((8, 128), F32),
            dma((STAGES,)),
            dma((2,)),
            dma((STAGES,)),
            dma((STAGES,)),
            dma((4,)),
            dma((4,)),
            dma((4,)),
            dma((UNITS, 3)),
            dma((2,)),
            dma((CHUNKS, 3)),
            dma((STAGES,)),
            dma((STAGES,)),
            dma((2,)),
            dma((3,)),
        ],
        compiler_params=pltpu.CompilerParams(
            collective_id=0, has_side_effects=True, vmem_limit_bytes=63 * 2**20
        ),
        name="routed_backward",
    )(
        expert_ids.T,
        slots.T,
        gates.T,
        tokens,
        grad_out,
        w_gate,
        w_up,
        w_down,
    )
    ret = ret.reshape(STAGES, 256, cw // 2)
    gt, gg, og, ou, od = pl.pallas_call(
        finish,
        in_specs=[any_spec] * 6,
        out_specs=(any_spec,) * 5,
        out_shape=(
            sds(tokens.shape, BF16),
            sds((8, 128), F32),
            sds(w_gate.shape, BF16),
            sds(w_up.shape, BF16),
            sds(w_down.shape, BF16),
        ),
        scratch_shapes=[
            vm((8, 128), F32),
            vm((512, 256), BF16),
            vm((STAGES, 256, cw // 2), BF16),
            vm(tokens.shape, BF16),
            vm((3,) + w_gate.shape[1:], BF16),
            dma((3,)),
            dma((3, 7)),
            dma((3, 7)),
            dma((STAGES + 1,)),
        ],
        compiler_params=pltpu.CompilerParams(vmem_limit_bytes=62 * 2**20),
        name="finish",
    )(placet, gg, ret, og, ou, od)
    return (gt, gg.T, og, ou, od)


def solution(mesh):
    rows = P(("wide", "narrow"), None)
    weights = P("wide", "narrow", None)
    return jax.shard_map(
        per_device,
        mesh=mesh,
        in_specs=(rows,) * 5 + (weights,) * 3,
        out_specs=(rows, rows, weights, weights, weights),
        check_vma=False,
    )
```

```python
import functools

import jax
import jax.numpy as jnp
from jax import lax
from jax.experimental import pallas as pl
from jax.experimental.pallas import tpu as pltpu
from jax.sharding import PartitionSpec as P

CAP = 4
WIDE = 16
NARROW = 8
ROWS = WIDE * CAP
STAGES = 7
CHUNKS = 2 * STAGES
UNITS = 2 * CHUNKS
GATHER_LAG = (2, 4, 6)
RING = 14
REDUCE_LAG = (4, 8, 11)
GRADS_LAG = 4
PAD = 256
MESH = pl.DeviceIdType.MESH
F32 = jnp.float32
BF16 = jnp.bfloat16


def dot(left, right):
    return jnp.dot(left, right, preferred_element_type=F32)


def dot_nt(left, right):
    return lax.dot_general(left, right, (((1,), (1,)), ((), ())), preferred_element_type=F32)


def iota(shape, dim):
    return lax.broadcasted_iota(jnp.int32, shape, dim)


def gather_is_b(unit):
    return (unit * 11) % 28 < 11


def reduce_is_b(chunk):
    return (chunk * 5 + 9) % 14 < 5


def kernel(
    ids_ref,
    slots_ref,
    gates_ref,
    tok_hbm,
    cot_hbm,
    wg_hbm,
    wu_hbm,
    wd_hbm,
    og_hbm,
    ou_hbm,
    od_hbm,
    placet_hbm,
    ret_hbm,
    gg_hbm,
    place,
    place_t,
    tokbuf,
    sendbuf,
    a2abuf,
    xbuf,
    wab,
    wdn,
    acc_ab,
    acc_u,
    gsend,
    ga2a,
    gbuf,
    dd,
    dd_t,
    hq_t,
    pbuf,
    rb,
    fin,
    rbuf,
    retsend,
    qbuf,
    stage_ab,
    stage_d,
    gp,
    gpr,
    gsum,
    gret,
    gg_ref,
    tok_sem,
    w_sem,
    a2a_s,
    a2a_r,
    g_s,
    g_r,
    ag_s,
    ag_r,
    c_s,
    c_r,
    ret_s,
    ret_r,
    grad_sem,
    out_sem,
):
    w = lax.axis_index("wide")
    n = lax.axis_index("narrow")
    y, xh = n // 2, n % 2
    yp, ym, y2 = (y + 1) % 4, (y + 3) % 4, (y + 2) % 4
    ox = 1 - xh
    cw = xbuf.shape[3]
    qw = cw // 2
    sw = 2 * cw
    hid = wg_hbm.shape[1]

    def at(yy, xx):
        return yy * 2 + xx

    xl, core = (w // 2) % 2, w % 2

    def swap(source, expert):
        return (((source // 2) % 2) ^ ((expert // 2) % 2)) & (source % 2)

    dev_p, dev_m, dev_x = at(yp, xh), at(ym, xh), at(y, ox)

    def cols(chunk):
        return pl.ds(pl.multiple_of(chunk * cw, 128), cw)

    def remote(src, dst, ss, rs, to_w, to_n):
        return pltpu.make_async_remote_copy(
            src_ref=src,
            dst_ref=dst,
            send_sem=ss,
            recv_sem=rs,
            device_id=(to_w, to_n),
            device_id_type=MESH,
        )

    barrier = pltpu.get_barrier_semaphore()

    @pl.loop(1, WIDE)
    def _(i):
        pl.semaphore_signal(barrier, inc=1, device_id=((w + i) % WIDE, n), device_id_type=MESH)

    @pl.loop(0, WIDE)
    def _(i):
        pl.semaphore_signal(barrier, inc=1, device_id=(i, at(y, ox)), device_id_type=MESH)

    @pl.loop(1, 4)
    def _(i):
        for xx in range(2):
            pl.semaphore_signal(
                barrier, inc=1, device_id=(w, at((y + i) % 4, xx)), device_id_type=MESH
            )

    def tok_copy(g, arr):
        src = tok_hbm if arr == 0 else cot_hbm
        span = pl.ds(pl.multiple_of(g * sw, 128), sw)
        return pltpu.make_async_copy(src.at[:, span], tokbuf.at[g, arr], tok_sem.at[g])

    @pl.loop(0, STAGES)
    def _(g):
        for arr in range(2):
            tok_copy(g, arr).start()

    def w_copies(chunk):
        return (
            pltpu.make_async_copy(
                wg_hbm.at[0, :, cols(chunk)], wab.at[chunk, pl.ds(0, hid)], w_sem.at[0]
            ),
            pltpu.make_async_copy(
                wu_hbm.at[0, :, cols(chunk)], wab.at[chunk, pl.ds(PAD, hid)], w_sem.at[0]
            ),
            pltpu.make_async_copy(
                wd_hbm.at[0, :, cols(chunk)], wdn.at[chunk, pl.ds(0, hid)], w_sem.at[1]
            ),
        )

    def landed(ref, sem):
        remote(ref, ref, sem, sem, w, n ^ 1).wait_recv()

    def sent(ref, sem):
        remote(ref, ref, sem, sem, w, n ^ 1).wait_send()

    def here(ref, sem):
        pltpu.make_async_copy(ref, ref, sem).wait()

    kept = (ids_ref[...] < WIDE) & (slots_ref[...] < CAP)
    target = jnp.where(kept, ids_ref[...] * CAP + slots_ref[...], ROWS)
    row = iota((256, 128), 0)
    code = (row >> 4) * CAP + (row & 3)
    gates = gates_ref[...].astype(F32)
    hit = jnp.zeros((256, 128), F32)
    weight = jnp.zeros((256, 128), F32)
    for k in range(8):
        match = target[k : k + 1, :] == code
        hit = hit + jnp.where(match, 1.0, 0.0)
        weight = weight + jnp.where(match, gates[k : k + 1, :], 0.0)
    for q in range(4):
        part = jnp.where(((row >> 2) & 3) == q, hit, 0.0)
        place[:, q * 128 : (q + 1) * 128] = part.astype(BF16)
        place_t[q * 128 : (q + 1) * 128, :] = part.T.astype(BF16)
    gsend[...] = (
        dot(weight.astype(BF16), jnp.ones((128, 128), BF16)).astype(BF16).reshape(WIDE, 16, 128)
    )

    def a2a_copy(g, i):
        e = (w + i) % WIDE
        return remote(
            sendbuf.at[g, e],
            a2abuf.at[g, w],
            a2a_s.at[g],
            a2a_r.at[g],
            e,
            at(y, xh ^ swap(w, e)),
        )

    def ga_copy(i):
        e = (w + i) % WIDE
        return remote(gsend.at[e], ga2a.at[w], g_s.at[0], g_r.at[0], e, at(y, xh ^ swap(w, e)))

    def pack(g):
        here(tokbuf.at[g], tok_sem.at[g])
        for arr in range(2):
            slab = jnp.concatenate(
                [tokbuf[g, arr, :, q * qw : (q + 1) * qw] for q in range(4)], axis=0
            )
            sendbuf[g, :, arr] = dot(place[...], slab).astype(BF16).reshape(WIDE, 16, qw)

    def post(g):
        @pl.loop(1, WIDE)
        def _(i):
            a2a_copy(g, i).start()

        a2abuf[g, w] = sendbuf[g, w]

    pack(0)
    pl.semaphore_wait(barrier, 2 * WIDE - 1 + NARROW - 2)
    post(0)

    @pl.loop(1, WIDE)
    def _(i):
        ga_copy(i).start()

    ga2a[w] = gsend[w]

    @pl.loop(0, CHUNKS)
    def _(chunk):
        for cp in w_copies(chunk):
            cp.start()
        wab[chunk, hid:PAD] = jnp.zeros((PAD - hid, cw), BF16)
        wab[chunk, PAD + hid :] = jnp.zeros((PAD - hid, cw), BF16)
        wdn[chunk, hid:] = jnp.zeros((PAD - hid, cw), BF16)

    placet_copy = pltpu.make_async_copy(place_t, placet_hbm, out_sem.at[0])
    placet_copy.start()
    acc_ab[...] = jnp.zeros_like(acc_ab)
    acc_u[...] = jnp.zeros_like(acc_u)

    r2, c2 = iota((256, 256), 0), iota((256, 256), 1)
    sort_rows = (
        ((r2 >> 6) == ((c2 >> 2) & 3)) & (((r2 >> 2) & 15) == (c2 >> 4)) & ((r2 & 3) == (c2 & 3))
    )
    sort_rows = jnp.where(sort_rows, 1.0, 0.0).astype(BF16)
    unsort_rows = (
        ((c2 >> 6) == ((r2 >> 2) & 3)) & (((c2 >> 2) & 15) == (r2 >> 4)) & ((c2 & 3) == (r2 & 3))
    )
    unsort_rows = jnp.where(unsort_rows, 1.0, 0.0).astype(BF16)

    def ag_copy(u, s, piece, to_n):
        ref = xbuf.at[u, piece]
        return remote(ref, ref, ag_s.at[u // 7], ag_r.at[u % RING, s], w, to_n)

    def ag_half(u, s, piece, lower, to_n):
        ref = xbuf.at[u, piece, pl.ds(0 if lower else 32, 32)]
        return remote(ref, ref, ag_s.at[u // 7], ag_r.at[u % RING, s], w, to_n)

    part = functools.partial

    def sends_a(u):
        return (
            (
                part(ag_copy, u, 0, n, dev_x),
                part(ag_copy, u, 1, n, dev_p),
                part(ag_copy, u, 1, n, dev_m),
            ),
            (part(ag_copy, u, 1, dev_x, dev_p), part(ag_copy, u, 1, dev_x, dev_m)),
            (part(ag_copy, u, 2, dev_m, dev_p), part(ag_copy, u, 2, at(yp, ox), dev_m)),
        )

    def sends_b(u):
        return (
            (
                part(ag_copy, u, 0, n, dev_p),
                part(ag_copy, u, 0, n, dev_m),
                part(ag_copy, u, 2, n, dev_x),
            ),
            (
                part(ag_half, u, 1, dev_m, True, dev_p),
                part(ag_half, u, 1, dev_p, False, dev_m),
                part(ag_copy, u, 2, dev_m, dev_x),
                part(ag_copy, u, 2, dev_p, dev_x),
            ),
            (part(ag_copy, u, 2, at(y2, xh), dev_x),),
        )

    def start_all(copies):
        for cp in copies:
            cp().start()

    def sort_stage(g):
        landed(a2abuf.at[g, pl.ds(0, WIDE - 1)], a2a_r.at[g])
        for arr in range(2):
            rows = dot(sort_rows, a2abuf[g, :, arr].reshape(256, qw)).astype(BF16)
            for q in range(4):
                xbuf[g * 4 + arr * 2 + q // 2, n, :, (q % 2) * qw : (q % 2 + 1) * qw] = rows[
                    q * ROWS : (q + 1) * ROWS
                ]

    def gg_copy(i):
        return remote(gbuf.at[n], gbuf.at[n], g_s.at[1], g_r.at[1], w, (n + i) % NARROW)

    pack(1)
    lag1, lag2, lag3 = GATHER_LAG

    @pl.loop(0, UNITS + lag3)
    def _(t):
        @pl.when(t < UNITS)
        def _():
            @pl.when(t % 4 == 0)
            def _():
                sort_stage(t // 4)

            @pl.when(gather_is_b(t))
            def _():
                start_all(sends_b(t)[0])

            @pl.when(jnp.logical_not(gather_is_b(t)))
            def _():
                start_all(sends_a(t)[0])

        @pl.when(t == 0)
        def _():
            post(1)

        @pl.when((t % 4 == 1) & (t // 4 + 2 < STAGES))
        def _():
            pack(t // 4 + 2)
            post(t // 4 + 2)

        @pl.when(t == 3)
        def _():
            landed(ga2a.at[pl.ds(0, WIDE - 1)], g_r.at[0])
            gbuf[n] = dot(sort_rows[0:ROWS], ga2a[...].reshape(256, 128)).astype(BF16)

            @pl.loop(1, NARROW)
            def _(i):
                gg_copy(i).start()

        @pl.when(t == lag3)
        def _():
            landed(gbuf.at[pl.ds(0, NARROW - 1)], g_r.at[1])
            here(wab.at[:, pl.ds(0, 2 * hid)], w_sem.at[0])
            here(wdn.at[:, pl.ds(0, hid)], w_sem.at[1])

        u1 = t - lag1

        @pl.when((u1 >= 0) & (u1 < UNITS))
        def _():
            @pl.when(gather_is_b(u1))
            def _():
                landed(xbuf.at[u1, pl.ds(0, 2)], ag_r.at[u1 % RING, 0])
                start_all(sends_b(u1)[1])

            @pl.when(jnp.logical_not(gather_is_b(u1)))
            def _():
                landed(xbuf.at[u1, 0], ag_r.at[u1 % RING, 0])
                start_all(sends_a(u1)[1])

        u2 = t - lag2

        @pl.when((u2 >= 0) & (u2 < UNITS))
        def _():
            @pl.when(gather_is_b(u2))
            def _():
                landed(xbuf.at[u2, 0], ag_r.at[u2 % RING, 1])
                start_all(sends_b(u2)[2])

            @pl.when(jnp.logical_not(gather_is_b(u2)))
            def _():
                landed(xbuf.at[u2, pl.ds(0, 4)], ag_r.at[u2 % RING, 1])
                start_all(sends_a(u2)[2])

        u3 = t - lag3

        @pl.when(u3 >= 0)
        def _():
            @pl.when(gather_is_b(u3))
            def _():
                landed(xbuf.at[u3, pl.ds(0, 4)], ag_r.at[u3 % RING, 2])

            @pl.when(jnp.logical_not(gather_is_b(u3)))
            def _():
                landed(xbuf.at[u3, pl.ds(0, 2)], ag_r.at[u3 % RING, 2])

            chunk = (u3 // 4) * 2 + u3 % 2
            is_cot = (u3 // 2) % 2 == 1

            @pl.when(is_cot)
            def _():
                acc_u[...] += dot_nt(xbuf[u3].reshape(512, cw), wdn[chunk])

            @pl.when(jnp.logical_not(is_cot))
            def _():
                acc_ab[...] += dot_nt(xbuf[u3].reshape(512, cw), wab[chunk])

    def hidden(r):
        span = slice(r * 128, (r + 1) * 128)
        g = gbuf[2 * r : 2 * r + 2].reshape(128, 128).astype(F32)
        g = jnp.concatenate([g, g], axis=1)
        a = acc_ab[span, 0:PAD]
        b = acc_ab[span, PAD : 2 * PAD]
        u = acc_u[span, :]
        s = jax.nn.sigmoid(a)
        act = a * s
        dh = g * u
        da = dh * b * s * (1.0 + a * (1.0 - s))
        du = dh * act
        h = act * b
        dd[span, 0:PAD] = da.astype(BF16)
        dd[span, PAD : 2 * PAD] = du.astype(BF16)
        acc_ab[span, 0:PAD] = h
        acc_u[span, :] = u * h

    for r in range(4):
        hidden(r)

    def turn():
        gp[4:8] = jnp.zeros((4, 128), F32)
        for r in range(4):
            span = slice(r * 128, (r + 1) * 128)
            dd_t[:, span] = dd[span, :].astype(F32).T.astype(BF16)
            hq_t[:, span] = acc_ab[span, 0:PAD].T.astype(BF16)
            gp[r : r + 1, :] = jnp.sum(acc_u[span, :].T, axis=0, keepdims=True)
        gpr[n] = gp[...]

        @pl.loop(1, NARROW)
        def _(i):
            gp_copy(i).start()

    def gp_copy(i):
        return remote(gp, gpr.at[n], g_s.at[2], g_r.at[2], w, (n + i) % NARROW)

    def gr_copy(i):
        e = (w + i) % WIDE
        return remote(gsum, gret.at[w], g_s.at[3], g_r.at[3], e, n)

    lo, hi = pl.ds(0, 32), pl.ds(32, 32)

    def c_copy(k, s, piece, slot, to_n):
        return remote(
            pbuf.at[k, piece], rb.at[k, slot], c_s.at[k // 7], c_r.at[k, s], w, to_n
        )

    def c_half(k, s, piece, slot, span, to_n):
        return remote(
            pbuf.at[k, piece, span], rb.at[k, slot, span], c_s.at[k // 7], c_r.at[k, s], w, to_n
        )

    def add_into(k, piece, slot, span=slice(None)):
        pbuf[k, piece, span] = (
            pbuf[k, piece, span].astype(F32) + rb[k, slot, span].astype(F32)
        ).astype(BF16)

    def red_a(k):
        return (
            (
                part(c_copy, k, 0, at(y2, 0), 0, dev_p),
                part(c_copy, k, 0, at(y2, 1), 1, dev_m),
                part(c_copy, k, 1, at(yp, 1), 3, dev_p),
                part(c_copy, k, 1, at(ym, 0), 4, dev_m),
            ),
            (
                part(c_copy, k, 1, at(yp, 0), 2, dev_p),
                part(c_copy, k, 1, at(ym, 1), 5, dev_m),
            ),
            (part(c_copy, k, 2, at(y, ox), 6, dev_x),),
        )

    def red_b(k):
        return (
            tuple(part(c_copy, k, 0, at(yy, ox), yy, dev_x) for yy in range(4)),
            (
                part(c_half, k, 1, at(y2, xh), 4, lo, dev_p),
                part(c_half, k, 1, at(y2, xh), 4, hi, dev_m),
                part(c_half, k, 2, at(yp, xh), 5, hi, dev_p),
                part(c_half, k, 2, at(ym, xh), 6, lo, dev_m),
            ),
            (
                part(c_half, k, 2, at(yp, xh), 5, lo, dev_p),
                part(c_half, k, 2, at(ym, xh), 6, hi, dev_m),
            ),
        )

    def ret_copy(g, i):
        to = (w + i) % WIDE
        return remote(
            retsend.at[g, to],
            ret_hbm.at[g, w],
            ret_s.at[g],
            ret_r.at[g],
            to,
            at(y, xh ^ swap(to, w)),
        )

    def own_copy(g):
        return pltpu.make_async_copy(retsend.at[g, w], ret_hbm.at[g, w], out_sem.at[1])

    def grad_copies(k):
        slot = k % 2
        return (
            pltpu.make_async_copy(
                stage_ab.at[slot, pl.ds(0, hid)], og_hbm.at[0, :, cols(k)], grad_sem.at[slot]
            ),
            pltpu.make_async_copy(
                stage_ab.at[slot, pl.ds(PAD, hid)], ou_hbm.at[0, :, cols(k)], grad_sem.at[slot]
            ),
            pltpu.make_async_copy(
                stage_d.at[slot, pl.ds(0, hid)], od_hbm.at[0, :, cols(k)], grad_sem.at[slot]
            ),
        )

    gg_copy_out = pltpu.make_async_copy(gg_ref, gg_hbm, out_sem.at[2])

    def router():
        landed(gret.at[pl.ds(0, WIDE - 1)], g_r.at[3])

        row64 = iota((ROWS, WIDE), 0)
        spread = jnp.where((row64 >> 2) == iota((ROWS, WIDE), 1), 1.0, 0.0)
        line = gret[:, y, :]
        table = lax.dot_general(
            spread,
            line,
            (((1,), (0,)), ((), ())),
            precision=lax.Precision.HIGHEST,
            preferred_element_type=F32,
        )
        slot_row = iota((ROWS, 128), 0)
        turned = (((slot_row >> 3) & 1) ^ xl) & core
        lane = (xh ^ turned) * ROWS + w * CAP + (slot_row & 3)
        column = jnp.sum(
            jnp.where(iota((ROWS, 128), 1) == lane, table, 0.0), axis=1, keepdims=True
        )
        for k in range(8):
            match = target[k : k + 1, :] == slot_row
            gg_ref[k : k + 1, :] = jnp.sum(jnp.where(match, column, 0.0), axis=0, keepdims=True)
        gg_copy_out.start()

    clag1, clag2, clag3 = REDUCE_LAG

    @pl.loop(0, CHUNKS + clag3)
    def _(t):
        @pl.when(t < CHUNKS)
        def _():
            pbuf[t] = dot(dd[...], wab[t]).astype(BF16).reshape(NARROW, ROWS, cw)

            @pl.when(reduce_is_b(t))
            def _():
                start_all(red_b(t)[0])

            @pl.when(jnp.logical_not(reduce_is_b(t)))
            def _():
                start_all(red_a(t)[0])

        k1 = t - clag1

        @pl.when((k1 >= 0) & (k1 < CHUNKS))
        def _():
            @pl.when(reduce_is_b(k1))
            def _():
                landed(rb.at[k1, pl.ds(0, 4)], c_r.at[k1, 0])
                for yy in (y2, yp, ym):
                    add_into(k1, at(yy, xh), yy)
                start_all(red_b(k1)[1])
                fin[k1] = pbuf[k1, n].astype(F32) + rb[k1, y].astype(F32)

            @pl.when(jnp.logical_not(reduce_is_b(k1)))
            def _():
                landed(rb.at[k1, pl.ds(0, 2)], c_r.at[k1, 0])
                add_into(k1, at(yp, 0), 0)
                add_into(k1, at(ym, 1), 1)
                start_all(red_a(k1)[1])

        k2 = t - clag2

        @pl.when((k2 >= 0) & (k2 < CHUNKS))
        def _():
            @pl.when(reduce_is_b(k2))
            def _():
                landed(rb.at[k2, 4], c_r.at[k2, 1])
                add_into(k2, at(yp, xh), 4, lo)
                add_into(k2, at(ym, xh), 4, hi)
                start_all(red_b(k2)[2])

            @pl.when(jnp.logical_not(reduce_is_b(k2)))
            def _():
                landed(rb.at[k2, pl.ds(2, 4)], c_r.at[k2, 1])
                other = at(y, ox)
                pbuf[k2, other] = (
                    pbuf[k2, other].astype(F32)
                    + rb[k2, 2 + ox].astype(F32)
                    + rb[k2, 4 + ox].astype(F32)
                ).astype(BF16)
                start_all(red_a(k2)[2])
                fin[k2] = (
                    pbuf[k2, n].astype(F32)
                    + rb[k2, 2 + xh].astype(F32)
                    + rb[k2, 4 + xh].astype(F32)
                )

        k3 = t - clag3

        @pl.when(k3 >= 0)
        def _():
            @pl.when(reduce_is_b(k3))
            def _():
                landed(rb.at[k3, pl.ds(5, 2)], c_r.at[k3, 2])
                rbuf[k3] = (
                    fin[k3] + rb[k3, 5].astype(F32) + rb[k3, 6].astype(F32)
                ).astype(BF16)

            @pl.when(jnp.logical_not(reduce_is_b(k3)))
            def _():
                landed(rb.at[k3, 6], c_r.at[k3, 2])
                rbuf[k3] = (fin[k3] + rb[k3, 6].astype(F32)).astype(BF16)

            @pl.when(k3 % 2 == 1)
            def _():
                g = k3 // 2
                rows = jnp.concatenate(
                    [
                        rbuf[2 * g + q // 2, :, (q % 2) * qw : (q % 2 + 1) * qw]
                        for q in range(4)
                    ],
                    axis=0,
                )
                retsend[g] = dot(unsort_rows, rows).astype(BF16).reshape(WIDE, 16, qw)

                @pl.loop(1, WIDE)
                def _(i):
                    ret_copy(g, i).start()

                own_copy(g).start()

        @pl.when(t == 3)
        def _():
            turn()

        @pl.when(t == CHUNKS + 4)
        def _():
            router()

        kw = t - GRADS_LAG

        @pl.when((kw >= 0) & (kw < CHUNKS))
        def _():
            slot = kw % 2

            @pl.when(kw >= 2)
            def _():
                for cp in grad_copies(kw):
                    cp.wait()

            unit = (kw // 2) * 4 + kw % 2
            stage_ab[slot] = dot(dd_t[...], xbuf[unit].reshape(512, cw)).astype(BF16)

            @pl.loop(0, NARROW)
            def _(piece):
                g = gbuf[piece].astype(F32)
                g = jnp.concatenate([g] * (cw // 128), axis=1)
                qbuf[piece] = (g * xbuf[unit + 2, piece].astype(F32)).astype(BF16)

            stage_d[slot] = dot(hq_t[...], qbuf[...].reshape(512, cw)).astype(BF16)
            for cp in grad_copies(kw):
                cp.start()

        @pl.when(t == 9)
        def _():
            landed(gpr.at[pl.ds(0, NARROW - 1)], g_r.at[2])
            gsum[...] = jnp.sum(gpr[...], axis=0)
            gret[w] = gsum[...]

            @pl.loop(1, WIDE)
            def _(i):
                gr_copy(i).start()

    sent(gsend.at[pl.ds(0, WIDE - 1)], g_s.at[0])
    sent(gbuf.at[pl.ds(0, NARROW - 1)], g_s.at[1])
    sent(gpr.at[pl.ds(0, NARROW - 1)], g_s.at[2])
    sent(gret.at[pl.ds(0, WIDE - 1)], g_s.at[3])
    for i in range(4):
        sent(xbuf.at[pl.ds(i * 7, 7), pl.ds(0, 7)], ag_s.at[i])
    for i in range(2):
        sent(pbuf.at[pl.ds(i * 7, 7), pl.ds(0, 7)], c_s.at[i])
    for k in range(CHUNKS - 2, CHUNKS):
        for cp in grad_copies(k):
            cp.wait()
    placet_copy.wait()
    gg_copy_out.wait()

    @pl.loop(0, STAGES)
    def _(g):
        sent(sendbuf.at[g, pl.ds(0, WIDE - 1)], a2a_s.at[g])
        sent(retsend.at[g, pl.ds(0, WIDE - 1)], ret_s.at[g])
        landed(retsend.at[g, pl.ds(0, WIDE - 1)], ret_r.at[g])

    here(retsend.at[:, 0], out_sem.at[1])


def finish(
    placet_hbm,
    gg_in,
    ret_hbm,
    og_in,
    ou_in,
    od_in,
    gt_hbm,
    gg_out,
    og_hbm,
    ou_hbm,
    od_hbm,
    gg,
    placet,
    ret,
    gt,
    held,
    small_sem,
    in_sem,
    out_sem,
    gt_sem,
):
    qw = ret.shape[2]
    step = 32
    parts = held.shape[1] // step
    rows_in = (
        pltpu.make_async_copy(placet_hbm, placet, small_sem.at[0]),
        pltpu.make_async_copy(ret_hbm, ret, small_sem.at[1]),
        pltpu.make_async_copy(gg_in, gg, small_sem.at[2]),
    )
    loads, stores = [], []
    for i, (src, dst) in enumerate(((og_in, og_hbm), (ou_in, ou_hbm), (od_in, od_hbm))):
        for j in range(parts):
            span = pl.ds(j * step, step)
            here = held.at[i, span]
            loads.append(pltpu.make_async_copy(src.at[0, span], here, in_sem.at[i, j]))
            stores.append(pltpu.make_async_copy(here, dst.at[0, span], out_sem.at[i, j]))
    for cp in loads[:parts]:
        cp.start()
    for cp in rows_in:
        cp.start()
    for cp in loads[parts:]:
        cp.start()
    for load, store in zip(loads[:parts], stores[:parts]):
        load.wait()
        store.start()
    for cp in rows_in:
        cp.wait()
    homes = [pltpu.make_async_copy(gg, gg_out, gt_sem.at[STAGES])]
    homes[0].start()
    for g in range(STAGES):
        home = dot(placet[...], ret[g]).astype(BF16)
        for q in range(4):
            gt[:, (g * 4 + q) * qw : (g * 4 + q + 1) * qw] = home[q * 128 : (q + 1) * 128]
        span = pl.ds(g * 4 * qw, 4 * qw)
        homes.append(pltpu.make_async_copy(gt.at[:, span], gt_hbm.at[:, span], gt_sem.at[g]))
        homes[-1].start()
        for k in range(parts + 2 * g, parts + 2 * g + 2):
            loads[k].wait()
            stores[k].start()
    for cp in stores + homes:
        cp.wait()


def per_device(tokens, grad_out, gates, expert_ids, slots, w_gate, w_up, w_down):
    width = tokens.shape[1]
    cw = width // CHUNKS
    any_spec = pl.BlockSpec(memory_space=pl.ANY)
    vmem_spec = pl.BlockSpec(memory_space=pltpu.VMEM)
    vm = pltpu.VMEM
    dma = pltpu.SemaphoreType.DMA
    sds = jax.ShapeDtypeStruct
    og, ou, od, placet, ret, gg = pl.pallas_call(
        kernel,
        out_shape=(
            sds(w_gate.shape, BF16),
            sds(w_up.shape, BF16),
            sds(w_down.shape, BF16),
            sds((512, 256), BF16),
            sds((STAGES, WIDE, 16, cw // 2), BF16),
            sds((8, 128), F32),
        ),
        in_specs=[vmem_spec] * 3 + [any_spec] * 5,
        out_specs=(any_spec,) * 6,
        scratch_shapes=[
            vm((256, 512), BF16),
            vm((512, 256), BF16),
            vm((STAGES, 2, 128, 2 * cw), BF16),
            vm((STAGES, WIDE, 2, 16, cw // 2), BF16),
            vm((STAGES, WIDE, 2, 16, cw // 2), BF16),
            vm((UNITS, NARROW, ROWS, cw), BF16),
            vm((CHUNKS, 2 * PAD, cw), BF16),
            vm((CHUNKS, PAD, cw), BF16),
            vm((512, 2 * PAD), F32),
            vm((512, PAD), F32),
            vm((WIDE, 16, 128), BF16),
            vm((WIDE, 16, 128), BF16),
            vm((NARROW, ROWS, 128), BF16),
            vm((512, 2 * PAD), BF16),
            vm((2 * PAD, 512), BF16),
            vm((PAD, 512), BF16),
            vm((CHUNKS, NARROW, ROWS, cw), BF16),
            vm((CHUNKS, 7, ROWS, cw), BF16),
            vm((CHUNKS, ROWS, cw), F32),
            vm((CHUNKS, ROWS, cw), BF16),
            vm((STAGES, WIDE, 16, cw // 2), BF16),
            vm((NARROW, ROWS, cw), BF16),
            vm((2, 2 * PAD, cw), BF16),
            vm((2, PAD, cw), BF16),
            vm((8, 128), F32),
            vm((NARROW, 8, 128), F32),
            vm((8, 128), F32),
            vm((WIDE, 8, 128), F32),
            vm((8, 128), F32),
            dma((STAGES,)),
            dma((2,)),
            dma((STAGES,)),
            dma((STAGES,)),
            dma((4,)),
            dma((4,)),
            dma((4,)),
            dma((RING, 3)),
            dma((2,)),
            dma((CHUNKS, 3)),
            dma((STAGES,)),
            dma((STAGES,)),
            dma((2,)),
            dma((3,)),
        ],
        compiler_params=pltpu.CompilerParams(
            collective_id=0, has_side_effects=True, vmem_limit_bytes=63 * 2**20
        ),
        name="routed_backward",
    )(
        expert_ids.T,
        slots.T,
        gates.T,
        tokens,
        grad_out,
        w_gate,
        w_up,
        w_down,
    )
    ret = ret.reshape(STAGES, 256, cw // 2)
    gt, gg, og, ou, od = pl.pallas_call(
        finish,
        in_specs=[any_spec] * 6,
        out_specs=(any_spec,) * 5,
        out_shape=(
            sds(tokens.shape, BF16),
            sds((8, 128), F32),
            sds(w_gate.shape, BF16),
            sds(w_up.shape, BF16),
            sds(w_down.shape, BF16),
        ),
        scratch_shapes=[
            vm((8, 128), F32),
            vm((512, 256), BF16),
            vm((STAGES, 256, cw // 2), BF16),
            vm(tokens.shape, BF16),
            vm((3,) + w_gate.shape[1:], BF16),
            dma((3,)),
            dma((3, 7)),
            dma((3, 7)),
            dma((STAGES + 1,)),
        ],
        compiler_params=pltpu.CompilerParams(vmem_limit_bytes=62 * 2**20),
        name="finish",
    )(placet, gg, ret, og, ou, od)
    return (gt, gg.T, og, ou, od)


def solution(mesh):
    rows = P(("wide", "narrow"), None)
    weights = P("wide", "narrow", None)
    return jax.shard_map(
        per_device,
        mesh=mesh,
        in_specs=(rows,) * 5 + (weights,) * 3,
        out_specs=(rows, rows, weights, weights, weights),
        check_vma=False,
    )
```

```python
import functools

import jax
import jax.numpy as jnp
from jax import lax
from jax.experimental import pallas as pl
from jax.experimental.pallas import tpu as pltpu
from jax.sharding import PartitionSpec as P

CAP = 4
WIDE = 16
NARROW = 8
ROWS = WIDE * CAP
STAGES = 7
CHUNKS = 2 * STAGES
UNITS = 2 * CHUNKS
GATHER_LAG = (2, 4, 6)
RING = 14
REDUCE_LAG = (4, 8, 12)
GRADS_LAG = 4
PAD = 256
MESH = pl.DeviceIdType.MESH
F32 = jnp.float32
BF16 = jnp.bfloat16


def dot(left, right):
    return jnp.dot(left, right, preferred_element_type=F32)


def dot_nt(left, right):
    return lax.dot_general(left, right, (((1,), (1,)), ((), ())), preferred_element_type=F32)


def iota(shape, dim):
    return lax.broadcasted_iota(jnp.int32, shape, dim)


def gather_is_b(unit):
    return (unit * 11) % 28 < 11


def reduce_is_b(chunk):
    return (chunk * 5 + 9) % 14 < 5


def kernel(
    ids_ref,
    slots_ref,
    gates_ref,
    tok_hbm,
    cot_hbm,
    wg_hbm,
    wu_hbm,
    wd_hbm,
    og_hbm,
    ou_hbm,
    od_hbm,
    placet_hbm,
    ret_hbm,
    gg_hbm,
    place,
    place_t,
    tokbuf,
    sendbuf,
    a2abuf,
    xbuf,
    wab,
    wdn,
    acc_ab,
    acc_u,
    gsend,
    ga2a,
    gbuf,
    dd,
    dd_t,
    hq_t,
    pbuf,
    rb,
    fin,
    rbuf,
    retsend,
    qbuf,
    stage_ab,
    stage_d,
    gp,
    gpr,
    gsum,
    gret,
    gg_ref,
    tok_sem,
    w_sem,
    a2a_s,
    a2a_r,
    g_s,
    g_r,
    ag_s,
    ag_r,
    c_s,
    c_r,
    ret_s,
    ret_r,
    grad_sem,
    out_sem,
):
    w = lax.axis_index("wide")
    n = lax.axis_index("narrow")
    y, xh = n // 2, n % 2
    yp, ym, y2 = (y + 1) % 4, (y + 3) % 4, (y + 2) % 4
    ox = 1 - xh
    cw = xbuf.shape[3]
    qw = cw // 2
    sw = 2 * cw
    hid = wg_hbm.shape[1]

    def at(yy, xx):
        return yy * 2 + xx

    xl, core = (w // 2) % 2, w % 2

    def swap(source, expert):
        return (((source // 2) % 2) ^ ((expert // 2) % 2)) & (source % 2)

    dev_p, dev_m, dev_x = at(yp, xh), at(ym, xh), at(y, ox)

    def cols(chunk):
        return pl.ds(pl.multiple_of(chunk * cw, 128), cw)

    def remote(src, dst, ss, rs, to_w, to_n):
        return pltpu.make_async_remote_copy(
            src_ref=src,
            dst_ref=dst,
            send_sem=ss,
            recv_sem=rs,
            device_id=(to_w, to_n),
            device_id_type=MESH,
        )

    barrier = pltpu.get_barrier_semaphore()

    @pl.loop(1, WIDE)
    def _(i):
        pl.semaphore_signal(barrier, inc=1, device_id=((w + i) % WIDE, n), device_id_type=MESH)

    @pl.loop(0, WIDE)
    def _(i):
        pl.semaphore_signal(barrier, inc=1, device_id=(i, at(y, ox)), device_id_type=MESH)

    @pl.loop(1, 4)
    def _(i):
        for xx in range(2):
            pl.semaphore_signal(
                barrier, inc=1, device_id=(w, at((y + i) % 4, xx)), device_id_type=MESH
            )

    def tok_copy(g, arr):
        src = tok_hbm if arr == 0 else cot_hbm
        span = pl.ds(pl.multiple_of(g * sw, 128), sw)
        return pltpu.make_async_copy(src.at[:, span], tokbuf.at[g, arr], tok_sem.at[g])

    @pl.loop(0, STAGES)
    def _(g):
        for arr in range(2):
            tok_copy(g, arr).start()

    def w_copies(chunk):
        return (
            pltpu.make_async_copy(
                wg_hbm.at[0, :, cols(chunk)], wab.at[chunk, pl.ds(0, hid)], w_sem.at[0]
            ),
            pltpu.make_async_copy(
                wu_hbm.at[0, :, cols(chunk)], wab.at[chunk, pl.ds(PAD, hid)], w_sem.at[0]
            ),
            pltpu.make_async_copy(
                wd_hbm.at[0, :, cols(chunk)], wdn.at[chunk, pl.ds(0, hid)], w_sem.at[1]
            ),
        )

    def landed(ref, sem):
        remote(ref, ref, sem, sem, w, n ^ 1).wait_recv()

    def sent(ref, sem):
        remote(ref, ref, sem, sem, w, n ^ 1).wait_send()

    def here(ref, sem):
        pltpu.make_async_copy(ref, ref, sem).wait()

    kept = (ids_ref[...] < WIDE) & (slots_ref[...] < CAP)
    target = jnp.where(kept, ids_ref[...] * CAP + slots_ref[...], ROWS)
    row = iota((256, 128), 0)
    code = (row >> 4) * CAP + (row & 3)
    gates = gates_ref[...].astype(F32)
    hit = jnp.zeros((256, 128), F32)
    weight = jnp.zeros((256, 128), F32)
    for k in range(8):
        match = target[k : k + 1, :] == code
        hit = hit + jnp.where(match, 1.0, 0.0)
        weight = weight + jnp.where(match, gates[k : k + 1, :], 0.0)
    for q in range(4):
        part = jnp.where(((row >> 2) & 3) == q, hit, 0.0)
        place[:, q * 128 : (q + 1) * 128] = part.astype(BF16)
        place_t[q * 128 : (q + 1) * 128, :] = part.T.astype(BF16)
    gsend[...] = (
        dot(weight.astype(BF16), jnp.ones((128, 128), BF16)).astype(BF16).reshape(WIDE, 16, 128)
    )

    def a2a_copy(g, i):
        e = (w + i) % WIDE
        return remote(
            sendbuf.at[g, e],
            a2abuf.at[g, w],
            a2a_s.at[g],
            a2a_r.at[g],
            e,
            at(y, xh ^ swap(w, e)),
        )

    def ga_copy(i):
        e = (w + i) % WIDE
        return remote(gsend.at[e], ga2a.at[w], g_s.at[0], g_r.at[0], e, at(y, xh ^ swap(w, e)))

    def pack(g):
        here(tokbuf.at[g], tok_sem.at[g])
        for arr in range(2):
            slab = jnp.concatenate(
                [tokbuf[g, arr, :, q * qw : (q + 1) * qw] for q in range(4)], axis=0
            )
            sendbuf[g, :, arr] = dot(place[...], slab).astype(BF16).reshape(WIDE, 16, qw)

    def post(g):
        @pl.loop(1, WIDE)
        def _(i):
            a2a_copy(g, i).start()

        a2abuf[g, w] = sendbuf[g, w]

    pack(0)
    pl.semaphore_wait(barrier, 2 * WIDE - 1 + NARROW - 2)
    post(0)

    @pl.loop(1, WIDE)
    def _(i):
        ga_copy(i).start()

    ga2a[w] = gsend[w]

    @pl.loop(0, CHUNKS)
    def _(chunk):
        for cp in w_copies(chunk):
            cp.start()
        wab[chunk, hid:PAD] = jnp.zeros((PAD - hid, cw), BF16)
        wab[chunk, PAD + hid :] = jnp.zeros((PAD - hid, cw), BF16)
        wdn[chunk, hid:] = jnp.zeros((PAD - hid, cw), BF16)

    placet_copy = pltpu.make_async_copy(place_t, placet_hbm, out_sem.at[0])
    placet_copy.start()
    acc_ab[...] = jnp.zeros_like(acc_ab)
    acc_u[...] = jnp.zeros_like(acc_u)

    r2, c2 = iota((256, 256), 0), iota((256, 256), 1)
    sort_rows = (
        ((r2 >> 6) == ((c2 >> 2) & 3)) & (((r2 >> 2) & 15) == (c2 >> 4)) & ((r2 & 3) == (c2 & 3))
    )
    sort_rows = jnp.where(sort_rows, 1.0, 0.0).astype(BF16)
    unsort_rows = (
        ((c2 >> 6) == ((r2 >> 2) & 3)) & (((c2 >> 2) & 15) == (r2 >> 4)) & ((c2 & 3) == (r2 & 3))
    )
    unsort_rows = jnp.where(unsort_rows, 1.0, 0.0).astype(BF16)

    def ag_copy(u, s, piece, to_n):
        ref = xbuf.at[u, piece]
        return remote(ref, ref, ag_s.at[u // 7], ag_r.at[u % RING, s], w, to_n)

    def ag_half(u, s, piece, lower, to_n):
        ref = xbuf.at[u, piece, pl.ds(0 if lower else 32, 32)]
        return remote(ref, ref, ag_s.at[u // 7], ag_r.at[u % RING, s], w, to_n)

    part = functools.partial

    def sends_a(u):
        return (
            (
                part(ag_copy, u, 0, n, dev_x),
                part(ag_copy, u, 1, n, dev_p),
                part(ag_copy, u, 1, n, dev_m),
            ),
            (part(ag_copy, u, 1, dev_x, dev_p), part(ag_copy, u, 1, dev_x, dev_m)),
            (part(ag_copy, u, 2, dev_m, dev_p), part(ag_copy, u, 2, at(yp, ox), dev_m)),
        )

    def sends_b(u):
        return (
            (
                part(ag_copy, u, 0, n, dev_p),
                part(ag_copy, u, 0, n, dev_m),
                part(ag_copy, u, 2, n, dev_x),
            ),
            (
                part(ag_half, u, 1, dev_m, True, dev_p),
                part(ag_half, u, 1, dev_p, False, dev_m),
                part(ag_copy, u, 2, dev_m, dev_x),
                part(ag_copy, u, 2, dev_p, dev_x),
            ),
            (part(ag_copy, u, 2, at(y2, xh), dev_x),),
        )

    def start_all(copies):
        for cp in copies:
            cp().start()

    def sort_stage(g):
        landed(a2abuf.at[g, pl.ds(0, WIDE - 1)], a2a_r.at[g])
        for arr in range(2):
            rows = dot(sort_rows, a2abuf[g, :, arr].reshape(256, qw)).astype(BF16)
            for q in range(4):
                xbuf[g * 4 + arr * 2 + q // 2, n, :, (q % 2) * qw : (q % 2 + 1) * qw] = rows[
                    q * ROWS : (q + 1) * ROWS
                ]

    def gg_copy(i):
        return remote(gbuf.at[n], gbuf.at[n], g_s.at[1], g_r.at[1], w, (n + i) % NARROW)

    pack(1)
    lag1, lag2, lag3 = GATHER_LAG

    @pl.loop(0, UNITS + lag3)
    def _(t):
        @pl.when(t < UNITS)
        def _():
            @pl.when(t % 4 == 0)
            def _():
                sort_stage(t // 4)

            @pl.when(gather_is_b(t))
            def _():
                start_all(sends_b(t)[0])

            @pl.when(jnp.logical_not(gather_is_b(t)))
            def _():
                start_all(sends_a(t)[0])

        @pl.when(t == 0)
        def _():
            post(1)

        @pl.when((t % 4 == 1) & (t // 4 + 2 < STAGES))
        def _():
            pack(t // 4 + 2)
            post(t // 4 + 2)

        @pl.when(t == 3)
        def _():
            landed(ga2a.at[pl.ds(0, WIDE - 1)], g_r.at[0])
            gbuf[n] = dot(sort_rows[0:ROWS], ga2a[...].reshape(256, 128)).astype(BF16)

            @pl.loop(1, NARROW)
            def _(i):
                gg_copy(i).start()

        @pl.when(t == lag3)
        def _():
            landed(gbuf.at[pl.ds(0, NARROW - 1)], g_r.at[1])
            here(wab.at[:, pl.ds(0, 2 * hid)], w_sem.at[0])
            here(wdn.at[:, pl.ds(0, hid)], w_sem.at[1])

        u1 = t - lag1

        @pl.when((u1 >= 0) & (u1 < UNITS))
        def _():
            @pl.when(gather_is_b(u1))
            def _():
                landed(xbuf.at[u1, pl.ds(0, 2)], ag_r.at[u1 % RING, 0])
                start_all(sends_b(u1)[1])

            @pl.when(jnp.logical_not(gather_is_b(u1)))
            def _():
                landed(xbuf.at[u1, 0], ag_r.at[u1 % RING, 0])
                start_all(sends_a(u1)[1])

        u2 = t - lag2

        @pl.when((u2 >= 0) & (u2 < UNITS))
        def _():
            @pl.when(gather_is_b(u2))
            def _():
                landed(xbuf.at[u2, 0], ag_r.at[u2 % RING, 1])
                start_all(sends_b(u2)[2])

            @pl.when(jnp.logical_not(gather_is_b(u2)))
            def _():
                landed(xbuf.at[u2, pl.ds(0, 4)], ag_r.at[u2 % RING, 1])
                start_all(sends_a(u2)[2])

        u3 = t - lag3

        @pl.when(u3 >= 0)
        def _():
            @pl.when(gather_is_b(u3))
            def _():
                landed(xbuf.at[u3, pl.ds(0, 4)], ag_r.at[u3 % RING, 2])

            @pl.when(jnp.logical_not(gather_is_b(u3)))
            def _():
                landed(xbuf.at[u3, pl.ds(0, 2)], ag_r.at[u3 % RING, 2])

            chunk = (u3 // 4) * 2 + u3 % 2
            is_cot = (u3 // 2) % 2 == 1

            @pl.when(is_cot)
            def _():
                acc_u[...] += dot_nt(xbuf[u3].reshape(512, cw), wdn[chunk])

            @pl.when(jnp.logical_not(is_cot))
            def _():
                acc_ab[...] += dot_nt(xbuf[u3].reshape(512, cw), wab[chunk])

    def hidden(r):
        span = slice(r * 128, (r + 1) * 128)
        g = gbuf[2 * r : 2 * r + 2].reshape(128, 128).astype(F32)
        g = jnp.concatenate([g, g], axis=1)
        a = acc_ab[span, 0:PAD]
        b = acc_ab[span, PAD : 2 * PAD]
        u = acc_u[span, :]
        s = jax.nn.sigmoid(a)
        act = a * s
        dh = g * u
        da = dh * b * s * (1.0 + a * (1.0 - s))
        du = dh * act
        h = act * b
        dd[span, 0:PAD] = da.astype(BF16)
        dd[span, PAD : 2 * PAD] = du.astype(BF16)
        acc_ab[span, 0:PAD] = h
        acc_u[span, :] = u * h

    for r in range(4):
        hidden(r)

    def turn():
        gp[4:8] = jnp.zeros((4, 128), F32)
        for r in range(4):
            span = slice(r * 128, (r + 1) * 128)
            dd_t[:, span] = dd[span, :].astype(F32).T.astype(BF16)
            hq_t[:, span] = acc_ab[span, 0:PAD].T.astype(BF16)
            gp[r : r + 1, :] = jnp.sum(acc_u[span, :].T, axis=0, keepdims=True)
        gpr[n] = gp[...]

        @pl.loop(1, NARROW)
        def _(i):
            gp_copy(i).start()

    def gp_copy(i):
        return remote(gp, gpr.at[n], g_s.at[2], g_r.at[2], w, (n + i) % NARROW)

    def gr_copy(i):
        e = (w + i) % WIDE
        return remote(gsum, gret.at[w], g_s.at[3], g_r.at[3], e, n)

    lo, hi = pl.ds(0, 32), pl.ds(32, 32)

    def c_copy(k, s, piece, slot, to_n):
        return remote(
            pbuf.at[k, piece], rb.at[k, slot], c_s.at[k // 7], c_r.at[k, s], w, to_n
        )

    def c_half(k, s, piece, slot, span, to_n):
        return remote(
            pbuf.at[k, piece, span], rb.at[k, slot, span], c_s.at[k // 7], c_r.at[k, s], w, to_n
        )

    def add_into(k, piece, slot, span=slice(None)):
        pbuf[k, piece, span] = (
            pbuf[k, piece, span].astype(F32) + rb[k, slot, span].astype(F32)
        ).astype(BF16)

    def red_a(k):
        return (
            (
                part(c_copy, k, 0, at(y2, 0), 0, dev_p),
                part(c_copy, k, 0, at(y2, 1), 1, dev_m),
                part(c_copy, k, 1, at(yp, 1), 3, dev_p),
                part(c_copy, k, 1, at(ym, 0), 4, dev_m),
            ),
            (
                part(c_copy, k, 1, at(yp, 0), 2, dev_p),
                part(c_copy, k, 1, at(ym, 1), 5, dev_m),
            ),
            (part(c_copy, k, 2, at(y, ox), 6, dev_x),),
        )

    def red_b(k):
        return (
            tuple(part(c_copy, k, 0, at(yy, ox), yy, dev_x) for yy in range(4)),
            (
                part(c_half, k, 1, at(y2, xh), 4, lo, dev_p),
                part(c_half, k, 1, at(y2, xh), 4, hi, dev_m),
                part(c_half, k, 2, at(yp, xh), 5, hi, dev_p),
                part(c_half, k, 2, at(ym, xh), 6, lo, dev_m),
            ),
            (
                part(c_half, k, 2, at(yp, xh), 5, lo, dev_p),
                part(c_half, k, 2, at(ym, xh), 6, hi, dev_m),
            ),
        )

    def ret_copy(g, i):
        to = (w + i) % WIDE
        return remote(
            retsend.at[g, to],
            ret_hbm.at[g, w],
            ret_s.at[g],
            ret_r.at[g],
            to,
            at(y, xh ^ swap(to, w)),
        )

    def own_copy(g):
        return pltpu.make_async_copy(retsend.at[g, w], ret_hbm.at[g, w], out_sem.at[1])

    def grad_copies(k):
        slot = k % 2
        return (
            pltpu.make_async_copy(
                stage_ab.at[slot, pl.ds(0, hid)], og_hbm.at[0, :, cols(k)], grad_sem.at[slot]
            ),
            pltpu.make_async_copy(
                stage_ab.at[slot, pl.ds(PAD, hid)], ou_hbm.at[0, :, cols(k)], grad_sem.at[slot]
            ),
            pltpu.make_async_copy(
                stage_d.at[slot, pl.ds(0, hid)], od_hbm.at[0, :, cols(k)], grad_sem.at[slot]
            ),
        )

    gg_copy_out = pltpu.make_async_copy(gg_ref, gg_hbm, out_sem.at[2])

    def router():
        landed(gret.at[pl.ds(0, WIDE - 1)], g_r.at[3])

        row64 = iota((ROWS, WIDE), 0)
        spread = jnp.where((row64 >> 2) == iota((ROWS, WIDE), 1), 1.0, 0.0)
        line = gret[:, y, :]
        table = lax.dot_general(
            spread,
            line,
            (((1,), (0,)), ((), ())),
            precision=lax.Precision.HIGHEST,
            preferred_element_type=F32,
        )
        slot_row = iota((ROWS, 128), 0)
        turned = (((slot_row >> 3) & 1) ^ xl) & core
        lane = (xh ^ turned) * ROWS + w * CAP + (slot_row & 3)
        column = jnp.sum(
            jnp.where(iota((ROWS, 128), 1) == lane, table, 0.0), axis=1, keepdims=True
        )
        for k in range(8):
            match = target[k : k + 1, :] == slot_row
            gg_ref[k : k + 1, :] = jnp.sum(jnp.where(match, column, 0.0), axis=0, keepdims=True)
        gg_copy_out.start()

    clag1, clag2, clag3 = REDUCE_LAG

    @pl.loop(0, CHUNKS + clag3)
    def _(t):
        @pl.when(t < CHUNKS)
        def _():
            pbuf[t] = dot(dd[...], wab[t]).astype(BF16).reshape(NARROW, ROWS, cw)

            @pl.when(reduce_is_b(t))
            def _():
                start_all(red_b(t)[0])

            @pl.when(jnp.logical_not(reduce_is_b(t)))
            def _():
                start_all(red_a(t)[0])

        k1 = t - clag1

        @pl.when((k1 >= 0) & (k1 < CHUNKS))
        def _():
            @pl.when(reduce_is_b(k1))
            def _():
                landed(rb.at[k1, pl.ds(0, 4)], c_r.at[k1, 0])
                for yy in (y2, yp, ym):
                    add_into(k1, at(yy, xh), yy)
                start_all(red_b(k1)[1])
                fin[k1] = pbuf[k1, n].astype(F32) + rb[k1, y].astype(F32)

            @pl.when(jnp.logical_not(reduce_is_b(k1)))
            def _():
                landed(rb.at[k1, pl.ds(0, 2)], c_r.at[k1, 0])
                add_into(k1, at(yp, 0), 0)
                add_into(k1, at(ym, 1), 1)
                start_all(red_a(k1)[1])

        k2 = t - clag2

        @pl.when((k2 >= 0) & (k2 < CHUNKS))
        def _():
            @pl.when(reduce_is_b(k2))
            def _():
                landed(rb.at[k2, 4], c_r.at[k2, 1])
                add_into(k2, at(yp, xh), 4, lo)
                add_into(k2, at(ym, xh), 4, hi)
                start_all(red_b(k2)[2])

            @pl.when(jnp.logical_not(reduce_is_b(k2)))
            def _():
                landed(rb.at[k2, pl.ds(2, 4)], c_r.at[k2, 1])
                other = at(y, ox)
                pbuf[k2, other] = (
                    pbuf[k2, other].astype(F32)
                    + rb[k2, 2 + ox].astype(F32)
                    + rb[k2, 4 + ox].astype(F32)
                ).astype(BF16)
                start_all(red_a(k2)[2])
                fin[k2] = (
                    pbuf[k2, n].astype(F32)
                    + rb[k2, 2 + xh].astype(F32)
                    + rb[k2, 4 + xh].astype(F32)
                )

        k3 = t - clag3

        @pl.when(k3 >= 0)
        def _():
            @pl.when(reduce_is_b(k3))
            def _():
                landed(rb.at[k3, pl.ds(5, 2)], c_r.at[k3, 2])
                rbuf[k3] = (
                    fin[k3] + rb[k3, 5].astype(F32) + rb[k3, 6].astype(F32)
                ).astype(BF16)

            @pl.when(jnp.logical_not(reduce_is_b(k3)))
            def _():
                landed(rb.at[k3, 6], c_r.at[k3, 2])
                rbuf[k3] = (fin[k3] + rb[k3, 6].astype(F32)).astype(BF16)

            @pl.when(k3 % 2 == 1)
            def _():
                g = k3 // 2
                rows = jnp.concatenate(
                    [
                        rbuf[2 * g + q // 2, :, (q % 2) * qw : (q % 2 + 1) * qw]
                        for q in range(4)
                    ],
                    axis=0,
                )
                retsend[g] = dot(unsort_rows, rows).astype(BF16).reshape(WIDE, 16, qw)

                @pl.loop(1, WIDE)
                def _(i):
                    ret_copy(g, i).start()

                own_copy(g).start()

        @pl.when(t == 3)
        def _():
            turn()

        @pl.when(t == CHUNKS + 4)
        def _():
            router()

        kw = t - GRADS_LAG

        @pl.when((kw >= 0) & (kw < CHUNKS))
        def _():
            slot = kw % 2

            @pl.when(kw >= 2)
            def _():
                for cp in grad_copies(kw):
                    cp.wait()

            unit = (kw // 2) * 4 + kw % 2
            stage_ab[slot] = dot(dd_t[...], xbuf[unit].reshape(512, cw)).astype(BF16)

            @pl.loop(0, NARROW)
            def _(piece):
                g = gbuf[piece].astype(F32)
                g = jnp.concatenate([g] * (cw // 128), axis=1)
                qbuf[piece] = (g * xbuf[unit + 2, piece].astype(F32)).astype(BF16)

            stage_d[slot] = dot(hq_t[...], qbuf[...].reshape(512, cw)).astype(BF16)
            for cp in grad_copies(kw):
                cp.start()

        @pl.when(t == 9)
        def _():
            landed(gpr.at[pl.ds(0, NARROW - 1)], g_r.at[2])
            gsum[...] = jnp.sum(gpr[...], axis=0)
            gret[w] = gsum[...]

            @pl.loop(1, WIDE)
            def _(i):
                gr_copy(i).start()

    sent(gsend.at[pl.ds(0, WIDE - 1)], g_s.at[0])
    sent(gbuf.at[pl.ds(0, NARROW - 1)], g_s.at[1])
    sent(gpr.at[pl.ds(0, NARROW - 1)], g_s.at[2])
    sent(gret.at[pl.ds(0, WIDE - 1)], g_s.at[3])
    for i in range(4):
        sent(xbuf.at[pl.ds(i * 7, 7), pl.ds(0, 7)], ag_s.at[i])
    for i in range(2):
        sent(pbuf.at[pl.ds(i * 7, 7), pl.ds(0, 7)], c_s.at[i])
    for k in range(CHUNKS - 2, CHUNKS):
        for cp in grad_copies(k):
            cp.wait()
    placet_copy.wait()
    gg_copy_out.wait()

    @pl.loop(0, STAGES)
    def _(g):
        sent(sendbuf.at[g, pl.ds(0, WIDE - 1)], a2a_s.at[g])
        sent(retsend.at[g, pl.ds(0, WIDE - 1)], ret_s.at[g])
        landed(retsend.at[g, pl.ds(0, WIDE - 1)], ret_r.at[g])

    here(retsend.at[:, 0], out_sem.at[1])


def finish(
    placet_hbm,
    gg_in,
    ret_hbm,
    og_in,
    ou_in,
    od_in,
    gt_hbm,
    gg_out,
    og_hbm,
    ou_hbm,
    od_hbm,
    gg,
    placet,
    ret,
    gt,
    held,
    small_sem,
    in_sem,
    out_sem,
    gt_sem,
):
    qw = ret.shape[2]
    step = 32
    parts = held.shape[1] // step
    rows_in = (
        pltpu.make_async_copy(placet_hbm, placet, small_sem.at[0]),
        pltpu.make_async_copy(ret_hbm, ret, small_sem.at[1]),
        pltpu.make_async_copy(gg_in, gg, small_sem.at[2]),
    )
    loads, stores = [], []
    for i, (src, dst) in enumerate(((og_in, og_hbm), (ou_in, ou_hbm), (od_in, od_hbm))):
        for j in range(parts):
            span = pl.ds(j * step, step)
            here = held.at[i, span]
            loads.append(pltpu.make_async_copy(src.at[0, span], here, in_sem.at[i, j]))
            stores.append(pltpu.make_async_copy(here, dst.at[0, span], out_sem.at[i, j]))
    for cp in loads[:parts]:
        cp.start()
    for cp in rows_in:
        cp.start()
    for cp in loads[parts:]:
        cp.start()
    for load, store in zip(loads[:parts], stores[:parts]):
        load.wait()
        store.start()
    for cp in rows_in:
        cp.wait()
    homes = [pltpu.make_async_copy(gg, gg_out, gt_sem.at[STAGES])]
    homes[0].start()
    for g in range(STAGES):
        home = dot(placet[...], ret[g]).astype(BF16)
        for q in range(4):
            gt[:, (g * 4 + q) * qw : (g * 4 + q + 1) * qw] = home[q * 128 : (q + 1) * 128]
        span = pl.ds(g * 4 * qw, 4 * qw)
        homes.append(pltpu.make_async_copy(gt.at[:, span], gt_hbm.at[:, span], gt_sem.at[g]))
        homes[-1].start()
        for k in range(parts + 2 * g, parts + 2 * g + 2):
            loads[k].wait()
            stores[k].start()
    for cp in stores + homes:
        cp.wait()


def per_device(tokens, grad_out, gates, expert_ids, slots, w_gate, w_up, w_down):
    width = tokens.shape[1]
    cw = width // CHUNKS
    any_spec = pl.BlockSpec(memory_space=pl.ANY)
    vmem_spec = pl.BlockSpec(memory_space=pltpu.VMEM)
    vm = pltpu.VMEM
    dma = pltpu.SemaphoreType.DMA
    sds = jax.ShapeDtypeStruct
    og, ou, od, placet, ret, gg = pl.pallas_call(
        kernel,
        out_shape=(
            sds(w_gate.shape, BF16),
            sds(w_up.shape, BF16),
            sds(w_down.shape, BF16),
            sds((512, 256), BF16),
            sds((STAGES, WIDE, 16, cw // 2), BF16),
            sds((8, 128), F32),
        ),
        in_specs=[vmem_spec] * 3 + [any_spec] * 5,
        out_specs=(any_spec,) * 6,
        scratch_shapes=[
            vm((256, 512), BF16),
            vm((512, 256), BF16),
            vm((STAGES, 2, 128, 2 * cw), BF16),
            vm((STAGES, WIDE, 2, 16, cw // 2), BF16),
            vm((STAGES, WIDE, 2, 16, cw // 2), BF16),
            vm((UNITS, NARROW, ROWS, cw), BF16),
            vm((CHUNKS, 2 * PAD, cw), BF16),
            vm((CHUNKS, PAD, cw), BF16),
            vm((512, 2 * PAD), F32),
            vm((512, PAD), F32),
            vm((WIDE, 16, 128), BF16),
            vm((WIDE, 16, 128), BF16),
            vm((NARROW, ROWS, 128), BF16),
            vm((512, 2 * PAD), BF16),
            vm((2 * PAD, 512), BF16),
            vm((PAD, 512), BF16),
            vm((CHUNKS, NARROW, ROWS, cw), BF16),
            vm((CHUNKS, 7, ROWS, cw), BF16),
            vm((CHUNKS, ROWS, cw), F32),
            vm((CHUNKS, ROWS, cw), BF16),
            vm((STAGES, WIDE, 16, cw // 2), BF16),
            vm((NARROW, ROWS, cw), BF16),
            vm((2, 2 * PAD, cw), BF16),
            vm((2, PAD, cw), BF16),
            vm((8, 128), F32),
            vm((NARROW, 8, 128), F32),
            vm((8, 128), F32),
            vm((WIDE, 8, 128), F32),
            vm((8, 128), F32),
            dma((STAGES,)),
            dma((2,)),
            dma((STAGES,)),
            dma((STAGES,)),
            dma((4,)),
            dma((4,)),
            dma((4,)),
            dma((RING, 3)),
            dma((2,)),
            dma((CHUNKS, 3)),
            dma((STAGES,)),
            dma((STAGES,)),
            dma((2,)),
            dma((3,)),
        ],
        compiler_params=pltpu.CompilerParams(
            collective_id=0, has_side_effects=True, vmem_limit_bytes=63 * 2**20
        ),
        name="routed_backward",
    )(
        expert_ids.T,
        slots.T,
        gates.T,
        tokens,
        grad_out,
        w_gate,
        w_up,
        w_down,
    )
    ret = ret.reshape(STAGES, 256, cw // 2)
    gt, gg, og, ou, od = pl.pallas_call(
        finish,
        in_specs=[any_spec] * 6,
        out_specs=(any_spec,) * 5,
        out_shape=(
            sds(tokens.shape, BF16),
            sds((8, 128), F32),
            sds(w_gate.shape, BF16),
            sds(w_up.shape, BF16),
            sds(w_down.shape, BF16),
        ),
        scratch_shapes=[
            vm((8, 128), F32),
            vm((512, 256), BF16),
            vm((STAGES, 256, cw // 2), BF16),
            vm(tokens.shape, BF16),
            vm((3,) + w_gate.shape[1:], BF16),
            dma((3,)),
            dma((3, 7)),
            dma((3, 7)),
            dma((STAGES + 1,)),
        ],
        compiler_params=pltpu.CompilerParams(vmem_limit_bytes=62 * 2**20),
        name="finish",
    )(placet, gg, ret, og, ou, od)
    return (gt, gg.T, og, ou, od)


def solution(mesh):
    rows = P(("wide", "narrow"), None)
    weights = P("wide", "narrow", None)
    return jax.shard_map(
        per_device,
        mesh=mesh,
        in_specs=(rows,) * 5 + (weights,) * 3,
        out_specs=(rows, rows, weights, weights, weights),
        check_vma=False,
    )
```
